32 devices in a mesh: groups: 2 (over y), patch: 4 (over z), section: 2 (over x), head: 2 (over core).
Axes of the slice: x: 2, y: 2, z: 4, core: 2. Of those that a mesh axis runs over, the one named last changes fastest.
Arguments:
- ctrl_hidden: bfloat16 [2048, 3072], P(('groups', 'patch'), ('section', 'head')), parts along dimension 0, may hold values from -6 to 6
- base_hidden: bfloat16 [2048, 3072], P(('groups', 'patch'), ('section', 'head')), parts along dimension 0, may hold values from -6 to 6
- ctrl_qkv_weight: bfloat16 [3072, 3, 512], P('patch', None, ('section', 'head')), may hold values from -0.109375 to 0.109375
- base_qkv_weight: bfloat16 [3072, 3, 512], P('patch', None, ('section', 'head')), may hold values from -0.109375 to 0.109375
- ctrl_out_weight: bfloat16 [512, 3072], P(('section', 'head')), may hold values from -0.25 to 0.25
- base_out_weight: bfloat16 [512, 3072], P(('section', 'head')), may hold values from -0.25 to 0.25
- ctrl_mod: float32 [3, 3072], replicated, may hold values from -3 to 3
- base_mod: float32 [3, 3072], replicated, may hold values from -3 to 3
- ctrl_qk_gain: float32 [2, 128], replicated, may hold values from 0.7 to 24
- base_qk_gain: float32 [2, 128], replicated, may hold values from 0.7 to 24
- ctrl_stale: bfloat16 [2, 2048, 512], P(None, ('groups', 'patch'), ('section', 'head')), parts along dimension 1, may hold values from -6 to 6
- base_stale: bfloat16 [2, 2048, 512], P(None, ('groups', 'patch'), ('section', 'head')), parts along dimension 1, may hold values from -6 to 6
- ctrl_text: bfloat16 [2, 512, 512], P(None, 'groups', ('section', 'head')), parts along dimension 1, may hold values from -6 to 6
- base_text: bfloat16 [2, 512, 512], P(None, 'groups', ('section', 'head')), parts along dimension 1, may hold values from -6 to 6
- ctrl_order: int32 [16], replicated, may hold values from 0 to 15, as said below
- base_order: int32 [16], replicated, may hold values from 0 to 15, as said below
- text_len: int32 [2], P('groups'), parts along dimension 0, may hold values from 128 to 256
Outputs:
- ctrl_out: bfloat16 [2048, 3072], P(('groups', 'patch'), ('section', 'head')), parts along dimension 0
- base_out: bfloat16 [2048, 3072], P(('groups', 'patch'), ('section', 'head')), parts along dimension 0
The draws below stay inside these ranges and needn't reach their ends.
There are 2 independent parts, one for each index of `groups`. The reference program is written for one: setup_inputs(seed, part) draws one part's arguments, and reference() takes and returns one part's arrays. A program takes and returns all parts, laid end to end along the dimension named above; an argument that names none is the same for every part. Nothing has to cross between parts.
Inputs may be any that keep to these rules, and one draw needn't show every extreme that they name: `ctrl_order`: a permutation of the 16 blocks. `base_order`: a permutation of the 16 blocks; each patch of the base layout holds exactly one block from each patch of the control layout.
All inputs are finite; a program needn't handle non-finite values.
Results may differ from the reference program's by a relative error of at most 0.012.
The reference program's roundings to bfloat16 on the way count: a program that leaves them out, or rounds other values in their place, can miss the bound.
Values may be sent and summed in bfloat16 or wider, within the bound.
A program may use at most 64 MiB of HBM per device.

```python
import math
import jax
import jax.numpy as jnp
from jax import lax

D = 3072
HD = 128
HEADS = 4
TOK_DEV = 256
BLK_DEV = 4
BLK = 64
NBLK = 16
NI = 1024
TXT = 256
N_PATCH = 4


def block_orders(key):
    owners = NBLK // BLK_DEV
    first = jax.random.permutation(jax.random.fold_in(key, 11), NBLK).astype(jnp.int32)
    shifts = jax.random.permutation(jax.random.fold_in(key, 12), owners)[:BLK_DEV].astype(jnp.int32)
    target = jnp.arange(owners, dtype=jnp.int32)[:, None]
    within = jnp.arange(BLK_DEV, dtype=jnp.int32)[None, :]
    source = (target - shifts[None, :]) % owners * BLK_DEV + within
    return (first, first[source.reshape(-1)])


def draw_ctrl_order(key, part):
    orders = block_orders(key)
    return orders[0]


def draw_base_order(key, part):
    orders = block_orders(key)
    return orders[1]


def draw_ctrl_qk_gain(key, part):
    key = jax.random.fold_in(key, 21)
    return jnp.exp(jax.random.uniform(key, (2, HD), jnp.float32, math.log(0.7), math.log(1.6)))


def draw_base_qk_gain(key, part):
    key = jax.random.fold_in(key, 22)
    return jnp.exp(jax.random.uniform(key, (2, HD), jnp.float32, math.log(0.7), math.log(1.6)))


def block_scale(stream_key, dims, shards, low, top_value):
    loudness, own = 1.0, jax.random.fold_in(stream_key, 6)
    for position, blocks in shards:
        draws = jnp.exp(jax.random.uniform(jax.random.fold_in(own, position), (blocks,), jnp.float32, low / len(shards), top_value / len(shards)))
        loudness = loudness * jnp.repeat(draws, dims[position] // blocks).reshape([-1 if axis == position else 1 for axis in range(len(dims))])
    return loudness


def scatter_about(rng, shape, scale, bound, pieces=(), kind=jnp.bfloat16):
    values = scale * jax.random.normal(rng, shape, jnp.float32)
    if pieces:
        values = values * block_scale(rng, shape, pieces, -0.22, 0.18)
    return jnp.clip(values, -bound, bound).astype(kind)


def setup_inputs(seed: int = 0, part: int = 0) -> dict:
    seeds = jax.random.split(jax.random.key(seed), 18)
    part_splits = jax.random.split(jax.random.fold_in(seeds[17], part), 18)
    return {
        "ctrl_hidden": scatter_about(part_splits[0], (NI, D), 1.0, 6.0, ((0, 4), (1, 4))),
        "base_hidden": scatter_about(part_splits[1], (NI, D), 1.0, 6.0, ((0, 4), (1, 4))),
        "ctrl_qkv_weight": scatter_about(seeds[2], (D, 3, HEADS * HD), D ** -0.5, 0.109375, ((0, 4), (2, 4))),
        "base_qkv_weight": scatter_about(seeds[3], (D, 3, HEADS * HD), D ** -0.5, 0.109375, ((0, 4), (2, 4))),
        "ctrl_out_weight": scatter_about(seeds[4], (HEADS * HD, D), (HEADS * HD) ** -0.5, 0.25, ((0, 4),)),
        "base_out_weight": scatter_about(seeds[5], (HEADS * HD, D), (HEADS * HD) ** -0.5, 0.25, ((0, 4),)),
        "ctrl_mod": scatter_about(seeds[6], (3, D), 0.6, 3.0, (), jnp.float32),
        "base_mod": scatter_about(seeds[7], (3, D), 0.6, 3.0, (), jnp.float32),
        "ctrl_qk_gain": draw_ctrl_qk_gain(jax.random.fold_in(seeds[17], 71), part),
        "base_qk_gain": draw_base_qk_gain(jax.random.fold_in(seeds[17], 71), part),
        "ctrl_stale": scatter_about(part_splits[10], (2, NI, HEADS * HD), 1.0, 6.0, ((1, 4), (2, 4))),
        "base_stale": scatter_about(part_splits[11], (2, NI, HEADS * HD), 1.0, 6.0, ((1, 4), (2, 4))),
        "ctrl_text": scatter_about(part_splits[12], (2, TXT, HEADS * HD), 1.0, 6.0, ((2, 4),)),
        "base_text": scatter_about(part_splits[13], (2, TXT, HEADS * HD), 1.0, 6.0, ((2, 4),)),
        "ctrl_order": draw_ctrl_order(jax.random.fold_in(seeds[17], 71), part),
        "base_order": draw_base_order(jax.random.fold_in(seeds[17], 71), part),
        "text_len": jax.random.randint(part_splits[16], (1,), TXT // 2, TXT + 1).astype(jnp.int32),
    }


def modulate(hidden, mod):
    values = hidden.astype(jnp.float32)
    center = lax.optimization_barrier(jnp.mean(values, axis=-1, keepdims=True))
    spread = lax.optimization_barrier(jnp.mean((values - center) ** 2, axis=-1, keepdims=True))
    normed = (values - center) * lax.rsqrt(spread + 1e-06)
    return (normed * (1.0 + mod[1]) + mod[0]).astype(jnp.bfloat16)

def rms_scale(values, gain):
    return values * lax.rsqrt(lax.optimization_barrier(jnp.mean(values * values, axis=-1, keepdims=True)) + 1e-06) * gain

def branch(hidden, qkv_weight, out_weight, mod, gain, stale, text, text_len):
    normed = modulate(hidden, mod)
    qkv = jnp.dot(normed, qkv_weight.reshape(D, 3 * HEADS * HD), preferred_element_type=jnp.float32)
    qkv = qkv.reshape(NI, 3, HEADS, HD)
    query = rms_scale(qkv[:, 0], gain[0]).astype(jnp.bfloat16)
    key_new = rms_scale(qkv[:, 1], gain[1]).astype(jnp.bfloat16)
    value_new = qkv[:, 2].astype(jnp.bfloat16)
    stale_keys = stale[0].reshape(NI, HEADS, HD)
    stale_values = stale[1].reshape(NI, HEADS, HD)
    text_keys = text[0].reshape(TXT, HEADS, HD)
    text_values = text[1].reshape(TXT, HEADS, HD)
    live = jnp.concatenate([jnp.arange(TXT, dtype=jnp.int32) < text_len[0], jnp.ones((NI,), bool)])

    def per_patch(index):
        start = (index * TOK_DEV).astype(jnp.int32)
        zero = jnp.zeros((), jnp.int32)
        own_keys = lax.dynamic_slice_in_dim(key_new, start, TOK_DEV, 0)
        own_values = lax.dynamic_slice_in_dim(value_new, start, TOK_DEV, 0)
        keys = lax.dynamic_update_slice(stale_keys, own_keys, (start, zero, zero))
        values = lax.dynamic_update_slice(stale_values, own_values, (start, zero, zero))
        keys = jnp.concatenate([text_keys, keys], axis=0)
        values = jnp.concatenate([text_values, values], axis=0)
        rows = lax.dynamic_slice_in_dim(query, start, TOK_DEV, 0)
        score = jnp.einsum('qhd,khd->hqk', rows.astype(jnp.float32), keys.astype(jnp.float32)) * HD ** (-0.5)
        score = jnp.where(live[None, None, :], score, -1e+30)
        top = lax.optimization_barrier(jnp.max(score, axis=-1, keepdims=True))
        expo = jnp.exp(score - top)
        total = lax.optimization_barrier(jnp.sum(expo, axis=-1))
        weights = lax.optimization_barrier(expo.astype(jnp.bfloat16)).astype(jnp.float32)
        mixed = jnp.einsum('hqk,khd->qhd', weights, values.astype(jnp.float32))
        return (mixed / jnp.transpose(total)[:, :, None]).astype(jnp.bfloat16)
    attn = lax.map(per_patch, jnp.arange(N_PATCH, dtype=jnp.int32)).reshape(NI, HEADS, HD)

    def add_head(index, total):
        head_rows = lax.dynamic_index_in_dim(attn, index, 1, keepdims=False)
        weight_rows = lax.dynamic_slice_in_dim(out_weight, index * HD, HD, 0)
        part = jnp.dot(head_rows, weight_rows, preferred_element_type=jnp.float32)
        return total + lax.optimization_barrier(part.astype(jnp.bfloat16)).astype(jnp.float32)
    return lax.fori_loop(0, HEADS, add_head, jnp.zeros((NI, D), jnp.float32))

def reference(ctrl_hidden, base_hidden, ctrl_qkv_weight, base_qkv_weight, ctrl_out_weight, base_out_weight, ctrl_mod, base_mod, ctrl_qk_gain, base_qk_gain, ctrl_stale, base_stale, ctrl_text, base_text, ctrl_order, base_order, text_len):
    ctrl_proj = branch(ctrl_hidden, ctrl_qkv_weight, ctrl_out_weight, ctrl_mod, ctrl_qk_gain, ctrl_stale, ctrl_text, text_len)
    ctrl_out = (ctrl_hidden.astype(jnp.float32) + ctrl_mod[2] * ctrl_proj).astype(jnp.bfloat16)
    inverse = jnp.zeros((NBLK,), jnp.int32).at[ctrl_order].set(jnp.arange(NBLK, dtype=jnp.int32))
    source = inverse[base_order]
    relaid = ctrl_out.reshape(NBLK, BLK, D)[source].reshape(NI, D)
    base_proj = branch(base_hidden, base_qkv_weight, base_out_weight, base_mod, base_qk_gain, base_stale, base_text, text_len)
    base_out = (base_hidden.astype(jnp.float32) + base_mod[2] * base_proj + relaid.astype(jnp.float32)).astype(jnp.bfloat16)
    return (ctrl_out, base_out)
```

```python
import functools

import jax
import jax.numpy as jnp
from jax import lax
from jax.experimental import pallas as pl
from jax.experimental.pallas import tpu as pltpu
from jax.sharding import PartitionSpec as P

F32 = jnp.float32
BF16 = jnp.bfloat16


def kernel(
    sizes,
    text_len,
    ctrl_order,
    base_order,
    hid0,
    hid1,
    w0,
    w1,
    wo0,
    wo1,
    mod0,
    mod1,
    gain0,
    gain1,
    stale0,
    stale1,
    text0,
    text1,
    out0,
    out1,
    hbuf,
    wbuf,
    kvbuf,
    psend,
    pbuf,
    hn,
    score_buf,
    blk_send,
    blk_buf,
    h_send,
    h_fwd,
    h_recv,
    w_send,
    w_recv,
    y_send,
    y_recv,
    kv_send,
    kv_recv,
    p_send,
    p_recv,
    b_send,
    b_recv,
):
    n_groups, n_patch, n_sec, n_head = sizes
    n_sh = n_sec * n_head
    hids, ws, wos = (hid0, hid1), (w0, w1), (wo0, wo1)
    mods, gains, stales, texts, outs = (
        (mod0, mod1),
        (gain0, gain1),
        (stale0, stale1),
        (text0, text1),
        (out0, out1),
    )
    rows, cols = hid0.shape
    head_size = stale0.shape[2]
    width = n_sh * cols
    blk = rows // n_patch
    g = lax.axis_index("groups")
    z = lax.axis_index("patch")
    x = lax.axis_index("section")
    c = lax.axis_index("head")
    me = x * n_head + c
    other = 1 - c

    def device(g_=None, z_=None, x_=None, c_=None):
        return (
            g if g_ is None else g_,
            z if z_ is None else z_,
            x if x_ is None else x_,
            c if c_ is None else c_,
        )

    def remote(src, dst, send, recv, dev):
        return pltpu.make_async_remote_copy(
            src_ref=src,
            dst_ref=dst,
            send_sem=send,
            recv_sem=recv,
            device_id=dev,
            device_id_type=pl.DeviceIdType.MESH,
        )

    def hid_copy(b, k):
        src = hids[b]
        if k == 0:
            dev = device(c_=other)
        else:
            dev = device(x_=lax.rem(x + k, n_sec))
        return remote(src, hbuf.at[b, me], h_send.at[b, k], h_recv.at[b, me], dev)

    def hid_start(b):
        for k in list(range(1, n_sec)) + [0]:
            hid_copy(b, k).start()
        hbuf[b, me] = hids[b][...]

    def hid_fwd_copy(b, k):
        j = lax.rem(x + n_sec - k, n_sec) * n_head + c
        return remote(
            hbuf.at[b, j], hbuf.at[b, j], h_fwd.at[b, k], h_recv.at[b, j], device(c_=other)
        )

    def hid_forward(b):
        for k in range(1, n_sec):
            copy = hid_fwd_copy(b, k)
            copy.wait_recv()
            copy.start()

    def hid_wait(b):
        for k in range(n_sec):
            j = lax.rem(x + n_sec - k, n_sec) * n_head + other
            remote(
                hbuf.at[b, j], hbuf.at[b, j], h_fwd.at[b, 0], h_recv.at[b, j], device(c_=other)
            ).wait_recv()

    def w_copy(b, t, side):
        j = z - t if side == 0 else z + t
        src = ws[b].at[g] if t == 0 else wbuf.at[b, j, g]
        dev = device(z_=z + 1 if side == 0 else z - 1)
        return remote(src, wbuf.at[b, j, g], w_send.at[b, side, t], w_recv.at[b, j], dev)

    def kv_copy(b, t, side):
        j = z - t if side == 0 else z + t
        src = stales[b] if t == 0 else kvbuf.at[b, j]
        dev = device(z_=z + 1 if side == 0 else z - 1)
        return remote(src, kvbuf.at[b, j], kv_send.at[b, side, t], kv_recv.at[b, j], dev)

    def sends(t, side):
        if side == 0:
            return (z - t >= 0) & (z + 1 < n_patch)
        return (z + t < n_patch) & (z - 1 >= 0)

    def receives(t, side):
        return z - t - 1 >= 0 if side == 0 else z + t + 1 < n_patch

    def y_copy(b, j):
        return remote(
            wbuf.at[b, j, g], wbuf.at[b, j, g], y_send.at[b, j], y_recv.at[b, j], device(g_=1 - g)
        )

    def chain_start(make, b, t):
        for side in range(2):

            @pl.when(sends(t, side))
            def _():
                make(b, t, side).start()

    def w_arrive(b, t):
        for side in range(2):

            @pl.when(receives(t, side))
            def _():
                j = z - t - 1 if side == 0 else z + t + 1
                copy = remote(
                    wbuf.at[b, j, g],
                    wbuf.at[b, j, g],
                    y_send.at[b, j],
                    w_recv.at[b, j],
                    device(g_=1 - g),
                )
                copy.wait_recv()

        if t + 1 < n_patch - 1:
            chain_start(w_copy, b, t + 1)
        for side in range(2):

            @pl.when(receives(t, side))
            def _():
                y_copy(b, z - t - 1 if side == 0 else z + t + 1).start()

    def kv_arrive(b, t):
        for side in range(2):

            @pl.when(receives(t, side))
            def _():
                j = z - t - 1 if side == 0 else z + t + 1
                remote(
                    kvbuf.at[b, j],
                    kvbuf.at[b, j],
                    kv_send.at[b, side, 0],
                    kv_recv.at[b, j],
                    device(g_=1 - g),
                ).wait_recv()

        if t + 1 < n_patch - 1:
            chain_start(kv_copy, b, t + 1)

    def w_wait(b):
        for k in range(1, n_patch):
            j = lax.rem(z + k, n_patch)
            remote(
                wbuf.at[b, j, 1 - g],
                wbuf.at[b, j, 1 - g],
                y_send.at[b, j],
                y_recv.at[b, j],
                device(g_=1 - g),
            ).wait_recv()

    def normalize(b):
        step = min(32, rows)
        mod = mods[b]

        def body(i, carry):
            at = pl.ds(pl.multiple_of(i * step, step), step)
            total = jnp.zeros((step, 1), F32)
            for s in range(n_sh):
                total += jnp.sum(hbuf[b, s, at, :].astype(F32), axis=1, keepdims=True)
            center = total * (1.0 / width)
            spread = jnp.zeros((step, 1), F32)
            for s in range(n_sh):
                diff = hbuf[b, s, at, :].astype(F32) - center
                spread += jnp.sum(diff * diff, axis=1, keepdims=True)
            inv = lax.rsqrt(spread * (1.0 / width) + 1e-06)
            for s in range(n_sh):
                normed = (hbuf[b, s, at, :].astype(F32) - center) * inv
                hn[s, at, :] = (normed * (1.0 + mod[n_sh + s]) + mod[s]).astype(BF16)
            return carry

        lax.fori_loop(0, rows // step, body, 0)

    def rms(values, gain):
        mean = jnp.mean(values * values, axis=-1, keepdims=True)
        return (values * lax.rsqrt(mean + 1e-06) * gain).astype(BF16)

    def project(b):
        half = ws[b].shape[1]

        def body(s, acc):
            for part in range(2):
                acc += jnp.dot(
                    hn[s, :, part * half : (part + 1) * half],
                    wbuf[b, s, part],
                    preferred_element_type=F32,
                )
            return acc

        qkv = lax.fori_loop(0, n_sh, body, jnp.zeros((rows, 3 * head_size), F32))
        gain = gains[b]
        query = rms(qkv[:, :head_size], gain[0:1, :])
        kvbuf[b, z, 0] = rms(qkv[:, head_size : 2 * head_size], gain[1:2, :])
        kvbuf[b, z, 1] = qkv[:, 2 * head_size :].astype(BF16)
        return query

    def attend(b, query):
        scale = head_size ** (-0.5)
        text = texts[b]

        def scores(keys):
            return (
                lax.dot_general(query, keys, (((1,), (1,)), ((), ())), preferred_element_type=F32)
                * scale
            )

        slots = text.shape[1]
        text_score = scores(text[0])
        spot = lax.broadcasted_iota(jnp.int32, (rows, slots), 1)
        text_score = jnp.where(spot < text_len[0], text_score, -1e30)
        top = jnp.max(text_score, axis=1, keepdims=True)

        def first(s, top):
            score = scores(kvbuf[b, s, 0])
            score_buf[s] = score
            return jnp.maximum(top, jnp.max(score, axis=1, keepdims=True))

        top = lax.fori_loop(0, n_patch, first, top)
        expo = jnp.exp(text_score - top)
        total = jnp.sum(expo, axis=1, keepdims=True)
        mixed = jnp.dot(expo.astype(BF16), text[1], preferred_element_type=F32)

        def second(s, carry):
            total, mixed = carry
            expo = jnp.exp(score_buf[s] - top)
            return (
                total + jnp.sum(expo, axis=1, keepdims=True),
                mixed + jnp.dot(expo.astype(BF16), kvbuf[b, s, 1], preferred_element_type=F32),
            )

        total, mixed = lax.fori_loop(0, n_patch, second, (total, mixed))
        return (mixed / total).astype(BF16)

    def p_copy(b, k):
        s = peer(k)
        return remote(
            psend.at[b, s],
            pbuf.at[b, me],
            p_send.at[b, s],
            p_recv.at[b, me],
            device(x_=s // n_head, c_=lax.rem(s, n_head)),
        )

    def peer(k):
        if k < n_sh - n_head:
            return lax.rem(x + 1 + k // n_head, n_sec) * n_head + lax.rem(c + k, n_head)
        return x * n_head + (other if k == n_sh - n_head else c)

    def out_part(b, attn, s):
        wo = wos[b]
        if len(wo.shape) == 3:
            weight = wo[s]
        else:
            weight = wo[:, pl.ds(pl.multiple_of(s * cols, cols), cols)]
        return jnp.dot(attn, weight, preferred_element_type=F32).astype(BF16)

    def out_start(b, attn):
        for k in range(n_sh - 1):
            s = peer(k)
            psend[b, s] = out_part(b, attn, s)
            p_copy(b, k).start()
        pbuf[b, me] = out_part(b, attn, me)

    def out_wait(b):
        for k in range(n_sh - 1):
            s = peer(k)
            remote(
                psend.at[b, s], pbuf.at[b, s], p_send.at[b, s], p_recv.at[b, s], device(c_=other)
            ).wait_recv()

    def gated(b, at):
        total = pbuf[b, 0, at, :].astype(F32)
        for s in range(1, n_sh):
            total += pbuf[b, s, at, :].astype(F32)
        return hids[b][at, :].astype(F32) + mods[b][2 * n_sh + me] * total

    def ctrl_finish():
        for d in range(n_patch):
            at = pl.ds(d * blk, blk)
            out0[at, :] = gated(0, at).astype(BF16)

    def b_copy(k):
        d = lax.rem(z + k, n_patch)
        return remote(blk_send.at[d], blk_buf.at[z], b_send.at[d], b_recv.at[z], device(z_=d))

    def equal(one, two):
        return (one == two).astype(F32)

    def relay_start():
        def block_for(d):
            def outer(j, block):
                def inner(i, found):
                    return found + equal(base_order[d * n_patch + i], ctrl_order[z * n_patch + j])

                found = lax.fori_loop(0, n_patch, inner, jnp.float32(0.0))
                at = pl.ds(pl.multiple_of(j * blk, blk), blk)
                return block + found * out0[at, :].astype(F32)

            return lax.fori_loop(0, n_patch, outer, jnp.zeros((blk, cols), F32)).astype(BF16)

        for k in range(1, n_patch):
            d = lax.rem(z + k, n_patch)
            blk_send[d] = block_for(d)
            b_copy(k).start()
        blk_buf[z] = block_for(z)

    def relay_wait():
        for k in range(1, n_patch):
            d = lax.rem(z + k, n_patch)
            remote(
                blk_send.at[d], blk_buf.at[d], b_send.at[d], b_recv.at[d], device(z_=d)
            ).wait_recv()

    def base_finish():
        for i in range(n_patch):
            at = pl.ds(i * blk, blk)

            def outer(s, block):
                def inner(j, found):
                    return found + equal(ctrl_order[s * n_patch + j], base_order[z * n_patch + i])

                found = lax.fori_loop(0, n_patch, inner, jnp.float32(0.0))
                return block + found * blk_buf[s].astype(F32)

            relaid = lax.fori_loop(0, n_patch, outer, jnp.zeros((blk, cols), F32))
            out1[at, :] = (gated(1, at) + relaid).astype(BF16)

    barrier = pltpu.get_barrier_semaphore()
    partners = [device(g_=1 - g)]
    partners += [device(z_=lax.rem(z + k, n_patch)) for k in range(1, n_patch)]
    for k in range(n_sh - 1):
        s = peer(k)
        partners.append(device(x_=s // n_head, c_=lax.rem(s, n_head)))
    for partner in partners:
        pl.semaphore_signal(
            barrier, inc=1, device_id=partner, device_id_type=pl.DeviceIdType.MESH
        )
    pl.semaphore_wait(barrier, len(partners))

    last = n_patch - 1
    chain_start(w_copy, 0, 0)
    hid_start(0)
    chain_start(kv_copy, 0, 0)
    wbuf[0, z] = ws[0][...]
    wbuf[1, z] = ws[1][...]
    hid_start(1)
    hid_forward(0)
    w_arrive(0, 0)
    kv_arrive(0, 0)
    chain_start(w_copy, 1, 0)
    for t in range(1, last):
        w_arrive(0, t)
        kv_arrive(0, t)
        if t == 1:
            hid_wait(0)
            normalize(0)
            hid_forward(1)
            chain_start(kv_copy, 1, 0)
    w_arrive(1, 0)
    w_wait(0)
    query = project(0)
    kv_arrive(1, 0)
    for t in range(1, last - 1):
        w_arrive(1, t)
        kv_arrive(1, t)
    out_start(0, attend(0, query))
    w_arrive(1, last - 1)
    kv_arrive(1, last - 1)
    hid_wait(1)
    normalize(1)
    out_wait(0)
    ctrl_finish()
    relay_start()
    w_wait(1)
    query = project(1)
    out_start(1, attend(1, query))
    relay_wait()
    out_wait(1)
    base_finish()

    for b in range(2):
        for k in range(n_sec):
            hid_copy(b, k).wait_send()
        for k in range(1, n_sec):
            hid_fwd_copy(b, k).wait_send()
        for t in range(last):
            for side in range(2):

                @pl.when(sends(t, side))
                def _():
                    w_copy(b, t, side).wait_send()
                    kv_copy(b, t, side).wait_send()

        for k in range(1, n_patch):
            y_copy(b, lax.rem(z + k, n_patch)).wait_send()
        for k in range(n_sh - 1):
            p_copy(b, k).wait_send()
    for k in range(1, n_patch):
        b_copy(k).wait_send()


def local(
    sizes,
    ctrl_hidden,
    base_hidden,
    ctrl_qkv_weight,
    base_qkv_weight,
    ctrl_out_weight,
    base_out_weight,
    ctrl_mod,
    base_mod,
    ctrl_qk_gain,
    base_qk_gain,
    ctrl_stale,
    base_stale,
    ctrl_text,
    base_text,
    ctrl_order,
    base_order,
    text_len,
):
    n_groups, n_patch, n_sec, n_head = sizes
    n_sh = n_sec * n_head
    rows, cols = ctrl_hidden.shape
    w_rows, _, head_size = ctrl_qkv_weight.shape
    blk = rows // n_patch

    def halves(weight):
        return weight.reshape(2, w_rows // 2, 3 * head_size)

    def by_columns(weight):
        if cols % 128 == 0:
            return weight
        return weight.reshape(weight.shape[0], n_sh, cols).transpose(1, 0, 2)

    def mod_rows(mod):
        return mod.reshape(3 * n_sh, 1, cols)

    smem = pl.BlockSpec(memory_space=pltpu.SMEM)
    vmem = pl.BlockSpec(memory_space=pltpu.VMEM)
    dma = pltpu.SemaphoreType.DMA
    out = jax.ShapeDtypeStruct((rows, cols), BF16)
    return pl.pallas_call(
        functools.partial(kernel, sizes),
        out_shape=(out, out),
        in_specs=[smem] * 3 + [vmem] * 14,
        out_specs=(vmem, vmem),
        scratch_shapes=[
            pltpu.VMEM((2, n_sh, rows, cols), BF16),
            pltpu.VMEM((2, n_patch, 2, w_rows // 2, 3 * head_size), BF16),
            pltpu.VMEM((2, n_patch, 2, rows, head_size), BF16),
            pltpu.VMEM((2, n_sh, rows, cols), BF16),
            pltpu.VMEM((2, n_sh, rows, cols), BF16),
            pltpu.VMEM((n_sh, rows, cols), BF16),
            pltpu.VMEM((n_patch, rows, rows), F32),
            pltpu.VMEM((n_patch, blk, cols), BF16),
            pltpu.VMEM((n_patch, blk, cols), BF16),
            dma((2, n_sec)),
            dma((2, n_sec)),
            dma((2, n_sh)),
            dma((2, 2, n_patch)),
            dma((2, n_patch)),
            dma((2, n_patch)),
            dma((2, n_patch)),
            dma((2, 2, n_patch)),
            dma((2, n_patch)),
            dma((2, n_sh)),
            dma((2, n_sh)),
            dma((n_patch,)),
            dma((n_patch,)),
        ],
        compiler_params=pltpu.CompilerParams(
            collective_id=0, has_side_effects=True, vmem_limit_bytes=52 * 1024 * 1024
        ),
    )(
        text_len,
        ctrl_order,
        base_order,
        ctrl_hidden,
        base_hidden,
        halves(ctrl_qkv_weight),
        halves(base_qkv_weight),
        by_columns(ctrl_out_weight),
        by_columns(base_out_weight),
        mod_rows(ctrl_mod),
        mod_rows(base_mod),
        ctrl_qk_gain,
        base_qk_gain,
        ctrl_stale,
        base_stale,
        ctrl_text,
        base_text,
    )


def solution(mesh):
    sizes = tuple(mesh.shape[name] for name in ("groups", "patch", "section", "head"))
    in_specs = (
        P(("groups", "patch"), ("section", "head")),
        P(("groups", "patch"), ("section", "head")),
        P("patch", None, ("section", "head")),
        P("patch", None, ("section", "head")),
        P(("section", "head"), None),
        P(("section", "head"), None),
        P(),
        P(),
        P(),
        P(),
        P(None, ("groups", "patch"), ("section", "head")),
        P(None, ("groups", "patch"), ("section", "head")),
        P(None, "groups", ("section", "head")),
        P(None, "groups", ("section", "head")),
        P(),
        P(),
        P("groups"),
    )
    out_specs = (
        P(("groups", "patch"), ("section", "head")),
        P(("groups", "patch"), ("section", "head")),
    )
    return jax.shard_map(
        functools.partial(local, sizes),
        mesh=mesh,
        in_specs=in_specs,
        out_specs=out_specs,
        check_vma=False,
    )
```

```python
import functools

import jax
import jax.numpy as jnp
from jax import lax
from jax.experimental import pallas as pl
from jax.experimental.pallas import tpu as pltpu
from jax.sharding import PartitionSpec as P

F32 = jnp.float32
BF16 = jnp.bfloat16
PARTS = 2


def kernel(
    sizes,
    text_len,
    ctrl_order,
    base_order,
    hid0,
    hid1,
    w0,
    w1,
    wo0,
    wo1,
    mod0,
    mod1,
    gain0,
    gain1,
    stale0,
    stale1,
    text0,
    text1,
    out0,
    out1,
    hbuf,
    wbuf,
    kvbuf,
    psend,
    pbuf,
    pair,
    hn,
    score_buf,
    blk_send,
    blk_buf,
    h_send,
    h_fwd,
    h_recv,
    w_send,
    w_recv,
    y_send,
    y_recv,
    kv_send,
    kv_recv,
    p_send,
    p_recv,
    pair_send,
    pair_recv,
    b_send,
    b_recv,
):
    n_groups, n_patch, n_sec, n_head = sizes
    n_sh = n_sec * n_head
    hids, ws, wos = (hid0, hid1), (w0, w1), (wo0, wo1)
    mods, gains, stales, texts, outs = (
        (mod0, mod1),
        (gain0, gain1),
        (stale0, stale1),
        (text0, text1),
        (out0, out1),
    )
    rows, cols = hid0.shape
    head_size = stale0.shape[2]
    width = n_sh * cols
    blk = rows // n_patch
    g = lax.axis_index("groups")
    z = lax.axis_index("patch")
    x = lax.axis_index("section")
    c = lax.axis_index("head")
    me = x * n_head + c
    other = 1 - c

    def device(g_=None, z_=None, x_=None, c_=None):
        return (
            g if g_ is None else g_,
            z if z_ is None else z_,
            x if x_ is None else x_,
            c if c_ is None else c_,
        )

    def remote(src, dst, send, recv, dev):
        return pltpu.make_async_remote_copy(
            src_ref=src,
            dst_ref=dst,
            send_sem=send,
            recv_sem=recv,
            device_id=dev,
            device_id_type=pl.DeviceIdType.MESH,
        )

    def hid_copy(b, k):
        src = hids[b]
        if k == 0:
            dev = device(c_=other)
        else:
            dev = device(x_=lax.rem(x + k, n_sec))
        return remote(src, hbuf.at[b, me], h_send.at[b, k], h_recv.at[b, me], dev)

    def hid_start(b):
        for k in list(range(1, n_sec)) + [0]:
            hid_copy(b, k).start()
        hbuf[b, me] = hids[b][...]

    def hid_fwd_copy(b, k):
        j = lax.rem(x + n_sec - k, n_sec) * n_head + c
        return remote(
            hbuf.at[b, j], hbuf.at[b, j], h_fwd.at[b, k], h_recv.at[b, j], device(c_=other)
        )

    def hid_forward(b):
        for k in range(1, n_sec):
            copy = hid_fwd_copy(b, k)
            copy.wait_recv()
            copy.start()

    def hid_wait(b):
        for k in range(n_sec):
            j = lax.rem(x + n_sec - k, n_sec) * n_head + other
            remote(
                hbuf.at[b, j], hbuf.at[b, j], h_fwd.at[b, 0], h_recv.at[b, j], device(c_=other)
            ).wait_recv()

    def w_copy(b, t, side):
        j = z - t if side == 0 else z + t
        src = ws[b].at[:, g] if t == 0 else wbuf.at[b, j, g]
        dev = device(z_=z + 1 if side == 0 else z - 1)
        return remote(src, wbuf.at[b, j, g], w_send.at[b, side, t], w_recv.at[b, j], dev)

    def kv_copy(b, t, side):
        j = z - t if side == 0 else z + t
        src = stales[b] if t == 0 else kvbuf.at[b, j]
        dev = device(z_=z + 1 if side == 0 else z - 1)
        return remote(src, kvbuf.at[b, j], kv_send.at[b, side, t], kv_recv.at[b, j], dev)

    def sends(t, side):
        if side == 0:
            return (z - t >= 0) & (z + 1 < n_patch)
        return (z + t < n_patch) & (z - 1 >= 0)

    def receives(t, side):
        return z - t - 1 >= 0 if side == 0 else z + t + 1 < n_patch

    def y_copy(b, j):
        return remote(
            wbuf.at[b, j, g], wbuf.at[b, j, g], y_send.at[b, j], y_recv.at[b, j], device(g_=1 - g)
        )

    def chain_start(make, b, t):
        for side in range(2):

            @pl.when(sends(t, side))
            def _():
                make(b, t, side).start()

    def w_arrive(b, t):
        for side in range(2):

            @pl.when(receives(t, side))
            def _():
                j = z - t - 1 if side == 0 else z + t + 1
                copy = remote(
                    wbuf.at[b, j, g],
                    wbuf.at[b, j, g],
                    y_send.at[b, j],
                    w_recv.at[b, j],
                    device(g_=1 - g),
                )
                copy.wait_recv()

        if t + 1 < n_patch - 1:
            chain_start(w_copy, b, t + 1)
        for side in range(2):

            @pl.when(receives(t, side))
            def _():
                y_copy(b, z - t - 1 if side == 0 else z + t + 1).start()

    def kv_arrive(b, t):
        for side in range(2):

            @pl.when(receives(t, side))
            def _():
                j = z - t - 1 if side == 0 else z + t + 1
                remote(
                    kvbuf.at[b, j],
                    kvbuf.at[b, j],
                    kv_send.at[b, side, 0],
                    kv_recv.at[b, j],
                    device(g_=1 - g),
                ).wait_recv()

        if t + 1 < n_patch - 1:
            chain_start(kv_copy, b, t + 1)

    def w_wait(b):
        for k in range(1, n_patch):
            j = lax.rem(z + k, n_patch)
            remote(
                wbuf.at[b, j, 1 - g],
                wbuf.at[b, j, 1 - g],
                y_send.at[b, j],
                y_recv.at[b, j],
                device(g_=1 - g),
            ).wait_recv()

    def mod_row(b, i, s):
        if len(mods[b].shape) == 3:
            return mods[b][i * n_sh + s]
        return mods[b][i : i + 1, pl.ds(pl.multiple_of(s * cols, cols), cols)]

    def normalize(b):
        step = min(32, rows)
        def body(i, carry):
            at = pl.ds(pl.multiple_of(i * step, step), step)
            total = jnp.zeros((step, 1), F32)
            for s in range(n_sh):
                total += jnp.sum(hbuf[b, s, at, :].astype(F32), axis=1, keepdims=True)
            center = total * (1.0 / width)
            spread = jnp.zeros((step, 1), F32)
            for s in range(n_sh):
                diff = hbuf[b, s, at, :].astype(F32) - center
                spread += jnp.sum(diff * diff, axis=1, keepdims=True)
            inv = lax.rsqrt(spread * (1.0 / width) + 1e-06)
            for s in range(n_sh):
                normed = (hbuf[b, s, at, :].astype(F32) - center) * inv
                hn[s, at, :] = (normed * (1.0 + mod_row(b, 1, s)) + mod_row(b, 0, s)).astype(BF16)
            return carry

        lax.fori_loop(0, rows // step, body, 0)

    def rms(values, gain):
        mean = jnp.mean(values * values, axis=-1, keepdims=True)
        return (values * lax.rsqrt(mean + 1e-06) * gain).astype(BF16)

    def project(b):
        half = ws[b].shape[2]

        def body(s, acc):
            for part in range(2):
                acc += jnp.dot(
                    hn[s, :, part * half : (part + 1) * half],
                    jnp.concatenate([wbuf[b, s, part, i] for i in range(3)], axis=1),
                    preferred_element_type=F32,
                )
            return acc

        qkv = lax.fori_loop(
            0, n_sh, body, jnp.zeros((rows, 3 * head_size), F32), unroll=n_sh <= 4
        )
        gain = gains[b]
        query = rms(qkv[:, :head_size], gain[0:1, :])
        kvbuf[b, z, 0] = rms(qkv[:, head_size : 2 * head_size], gain[1:2, :])
        kvbuf[b, z, 1] = qkv[:, 2 * head_size :].astype(BF16)
        return query

    def attend(b, query):
        scale = head_size ** (-0.5)
        text = texts[b]

        def scores(keys):
            return (
                lax.dot_general(query, keys, (((1,), (1,)), ((), ())), preferred_element_type=F32)
                * scale
            )

        slots = text.shape[1]
        text_score = scores(text[0])
        spot = lax.broadcasted_iota(jnp.int32, (query.shape[0], slots), 1)
        text_score = jnp.where(spot < text_len[0], text_score, -1e30)
        top = jnp.max(text_score, axis=1, keepdims=True)

        def first(s, top):
            score = scores(kvbuf[b, s, 0])
            score_buf[s] = score
            return jnp.maximum(top, jnp.max(score, axis=1, keepdims=True))

        top = lax.fori_loop(0, n_patch, first, top, unroll=n_patch <= 4)
        expo = jnp.exp(text_score - top)
        total = jnp.sum(expo, axis=1, keepdims=True)
        mixed = jnp.dot(expo.astype(BF16), text[1], preferred_element_type=F32)

        def second(s, carry):
            total, mixed = carry
            expo = jnp.exp(score_buf[s] - top)
            return (
                total + jnp.sum(expo, axis=1, keepdims=True),
                mixed + jnp.dot(expo.astype(BF16), kvbuf[b, s, 1], preferred_element_type=F32),
            )

        total, mixed = lax.fori_loop(
            0, n_patch, second, (total, mixed), unroll=n_patch <= 4
        )
        return (mixed / total).astype(BF16)

    piece = rows // PARTS

    def rows_of(r):
        return pl.ds(r * piece, piece)

    def section_of(k):
        return lax.rem(x + 1 + k, n_sec)

    def pair_copy(b, r, k):
        o = section_of(k)
        src = psend.at[b, o * n_head + other, rows_of(r)]
        dst = pair.at[b, o, rows_of(r)]
        return remote(src, dst, pair_send.at[b, r, o], pair_recv.at[b, r, o], device(c_=other))

    def p_copy(b, r, k):
        o = section_of(k)
        src = psend.at[b, o * n_head + c, rows_of(r)]
        dst = pbuf.at[b, x, rows_of(r)]
        return remote(src, dst, p_send.at[b, r, o], p_recv.at[b, r, x], device(x_=o))

    def out_part(b, attn, s):
        wo = wos[b]
        if len(wo.shape) == 3:
            weight = wo[s]
        else:
            weight = wo[:, pl.ds(pl.multiple_of(s * cols, cols), cols)]
        return jnp.dot(attn, weight, preferred_element_type=F32).astype(BF16)

    def out_start(b, r, attn):
        for k in range(n_sec):
            s = section_of(k) * n_head + other
            psend[b, s, rows_of(r), :] = out_part(b, attn, s)
            pair_copy(b, r, k).start()
        for k in range(n_sec - 1):
            o = section_of(k)
            mine = out_part(b, attn, o * n_head + c).astype(F32)
            pair_copy(b, r, k).wait_recv()
            total = mine + pair[b, o, rows_of(r), :].astype(F32)
            psend[b, o * n_head + c, rows_of(r), :] = total.astype(BF16)
            p_copy(b, r, k).start()
        pbuf[b, x, rows_of(r), :] = out_part(b, attn, me)

    def out_wait(b, r):
        pair_copy(b, r, n_sec - 1).wait_recv()
        for k in range(n_sec - 1):
            o = section_of(k)
            remote(
                pbuf.at[b, o, rows_of(r)],
                pbuf.at[b, o, rows_of(r)],
                p_send.at[b, r, o],
                p_recv.at[b, r, o],
                device(c_=other),
            ).wait_recv()

    def attend_out(b, query):
        for r in range(PARTS):
            out_start(b, r, attend(b, query[r * piece : (r + 1) * piece]))

    def gated(b, at):
        total = pair[b, x, at, :].astype(F32)
        for o in range(n_sec):
            total += pbuf[b, o, at, :].astype(F32)
        return hids[b][at, :].astype(F32) + mod_row(b, 2, me) * total

    def ctrl_finish():
        for d in range(n_patch):
            if d * PARTS % n_patch == 0:
                out_wait(0, d * PARTS // n_patch)
            at = pl.ds(d * blk, blk)
            out0[at, :] = gated(0, at).astype(BF16)

    def b_copy(k):
        d = lax.rem(z + k, n_patch)
        return remote(blk_send.at[d], blk_buf.at[z], b_send.at[d], b_recv.at[z], device(z_=d))

    def equal(one, two):
        return (one == two).astype(F32)

    def relay_start():
        def block_for(d):
            def outer(j, block):
                def inner(i, found):
                    return found + equal(base_order[d * n_patch + i], ctrl_order[z * n_patch + j])

                found = lax.fori_loop(0, n_patch, inner, jnp.float32(0.0))
                at = pl.ds(pl.multiple_of(j * blk, blk), blk)
                return block + found * out0[at, :].astype(F32)

            return lax.fori_loop(0, n_patch, outer, jnp.zeros((blk, cols), F32)).astype(BF16)

        for k in range(1, n_patch):
            d = lax.rem(z + k, n_patch)
            blk_send[d] = block_for(d)
            b_copy(k).start()
        blk_buf[z] = block_for(z)

    def relay_wait():
        for k in range(1, n_patch):
            d = lax.rem(z + k, n_patch)
            remote(
                blk_send.at[d], blk_buf.at[d], b_send.at[d], b_recv.at[d], device(z_=d)
            ).wait_recv()

    def base_finish():
        for i in range(n_patch):
            at = pl.ds(i * blk, blk)

            def outer(s, block):
                def inner(j, found):
                    return found + equal(ctrl_order[s * n_patch + j], base_order[z * n_patch + i])

                found = lax.fori_loop(0, n_patch, inner, jnp.float32(0.0))
                return block + found * blk_buf[s].astype(F32)

            relaid = lax.fori_loop(0, n_patch, outer, jnp.zeros((blk, cols), F32))
            if i * PARTS % n_patch == 0:
                out_wait(1, i * PARTS // n_patch)
            out1[at, :] = (gated(1, at) + relaid).astype(BF16)

    barrier = pltpu.get_barrier_semaphore()
    partners = [device(g_=1 - g)]
    partners += [device(z_=lax.rem(z + k, n_patch)) for k in range(1, n_patch)]
    partners += [device(x_=section_of(k)) for k in range(n_sec - 1)]
    partners.append(device(c_=other))
    for partner in partners:
        pl.semaphore_signal(
            barrier, inc=1, device_id=partner, device_id_type=pl.DeviceIdType.MESH
        )
    pl.semaphore_wait(barrier, len(partners))

    last = n_patch - 1
    chain_start(w_copy, 0, 0)
    hid_start(0)
    chain_start(kv_copy, 0, 0)
    for b in range(2):
        for part in range(2):
            wbuf[b, z, part] = ws[b][:, part]
    hid_start(1)
    hid_forward(0)
    w_arrive(0, 0)
    kv_arrive(0, 0)
    chain_start(w_copy, 1, 0)
    hid_wait(0)
    normalize(0)
    for t in range(1, last - 1):
        w_arrive(0, t)
        kv_arrive(0, t)
    hid_forward(1)
    w_arrive(1, 0)
    w_arrive(0, last - 1)
    w_wait(0)
    query = project(0)
    chain_start(kv_copy, 1, 0)
    for t in range(1, last - 1):
        w_arrive(1, t)
    kv_arrive(0, last - 1)
    attend_out(0, query)
    for t in range(last - 1):
        kv_arrive(1, t)
    hid_wait(1)
    normalize(1)
    w_arrive(1, last - 1)
    ctrl_finish()
    relay_start()
    w_wait(1)
    query = project(1)
    kv_arrive(1, last - 1)
    attend_out(1, query)
    relay_wait()
    base_finish()

    for b in range(2):
        for k in range(n_sec):
            hid_copy(b, k).wait_send()
        for k in range(1, n_sec):
            hid_fwd_copy(b, k).wait_send()
        for t in range(last):
            for side in range(2):

                @pl.when(sends(t, side))
                def _():
                    w_copy(b, t, side).wait_send()
                    kv_copy(b, t, side).wait_send()

        for k in range(1, n_patch):
            y_copy(b, lax.rem(z + k, n_patch)).wait_send()
        for k in range(n_sec - 1):
            for r in range(PARTS):
                p_copy(b, r, k).wait_send()
        for k in range(n_sec):
            for r in range(PARTS):
                pair_copy(b, r, k).wait_send()
    for k in range(1, n_patch):
        b_copy(k).wait_send()


def local(
    sizes,
    ctrl_hidden,
    base_hidden,
    ctrl_qkv_weight,
    base_qkv_weight,
    ctrl_out_weight,
    base_out_weight,
    ctrl_mod,
    base_mod,
    ctrl_qk_gain,
    base_qk_gain,
    ctrl_stale,
    base_stale,
    ctrl_text,
    base_text,
    ctrl_order,
    base_order,
    text_len,
):
    n_groups, n_patch, n_sec, n_head = sizes
    n_sh = n_sec * n_head
    rows, cols = ctrl_hidden.shape
    w_rows, _, head_size = ctrl_qkv_weight.shape
    blk = rows // n_patch

    def halves(weight):
        return weight.transpose(1, 0, 2).reshape(3, 2, w_rows // 2, head_size)

    def by_columns(weight):
        if cols % 128 == 0:
            return weight
        return weight.reshape(weight.shape[0], n_sh, cols).transpose(1, 0, 2)

    def mod_rows(mod):
        return mod if cols % 128 == 0 else mod.reshape(3 * n_sh, 1, cols)

    smem = pl.BlockSpec(memory_space=pltpu.SMEM)
    vmem = pl.BlockSpec(memory_space=pltpu.VMEM)
    dma = pltpu.SemaphoreType.DMA
    out = jax.ShapeDtypeStruct((rows, cols), BF16)
    return pl.pallas_call(
        functools.partial(kernel, sizes),
        out_shape=(out, out),
        in_specs=[smem] * 3 + [vmem] * 14,
        out_specs=(vmem, vmem),
        scratch_shapes=[
            pltpu.VMEM((2, n_sh, rows, cols), BF16),
            pltpu.VMEM((2, n_patch, 2, 3, w_rows // 2, head_size), BF16),
            pltpu.VMEM((2, n_patch, 2, rows, head_size), BF16),
            pltpu.VMEM((2, n_sh, rows, cols), BF16),
            pltpu.VMEM((2, n_sec, rows, cols), BF16),
            pltpu.VMEM((2, n_sec, rows, cols), BF16),
            pltpu.VMEM((n_sh, rows, cols), BF16),
            pltpu.VMEM((n_patch, rows // PARTS, rows), F32),
            pltpu.VMEM((n_patch, blk, cols), BF16),
            pltpu.VMEM((n_patch, blk, cols), BF16),
            dma((2, n_sec)),
            dma((2, n_sec)),
            dma((2, n_sh)),
            dma((2, 2, n_patch)),
            dma((2, n_patch)),
            dma((2, n_patch)),
            dma((2, n_patch)),
            dma((2, 2, n_patch)),
            dma((2, n_patch)),
            dma((2, PARTS, n_sec)),
            dma((2, PARTS, n_sec)),
            dma((2, PARTS, n_sec)),
            dma((2, PARTS, n_sec)),
            dma((n_patch,)),
            dma((n_patch,)),
        ],
        compiler_params=pltpu.CompilerParams(
            collective_id=0, has_side_effects=True, vmem_limit_bytes=52 * 1024 * 1024
        ),
    )(
        text_len,
        ctrl_order,
        base_order,
        ctrl_hidden,
        base_hidden,
        halves(ctrl_qkv_weight),
        halves(base_qkv_weight),
        by_columns(ctrl_out_weight),
        by_columns(base_out_weight),
        mod_rows(ctrl_mod),
        mod_rows(base_mod),
        ctrl_qk_gain,
        base_qk_gain,
        ctrl_stale,
        base_stale,
        ctrl_text,
        base_text,
    )


def solution(mesh):
    sizes = tuple(mesh.shape[name] for name in ("groups", "patch", "section", "head"))
    in_specs = (
        P(("groups", "patch"), ("section", "head")),
        P(("groups", "patch"), ("section", "head")),
        P("patch", None, ("section", "head")),
        P("patch", None, ("section", "head")),
        P(("section", "head"), None),
        P(("section", "head"), None),
        P(),
        P(),
        P(),
        P(),
        P(None, ("groups", "patch"), ("section", "head")),
        P(None, ("groups", "patch"), ("section", "head")),
        P(None, "groups", ("section", "head")),
        P(None, "groups", ("section", "head")),
        P(),
        P(),
        P("groups"),
    )
    out_specs = (
        P(("groups", "patch"), ("section", "head")),
        P(("groups", "patch"), ("section", "head")),
    )
    return jax.shard_map(
        functools.partial(local, sizes),
        mesh=mesh,
        in_specs=in_specs,
        out_specs=out_specs,
        check_vma=False,
    )
```

```python
import functools

import jax
import jax.numpy as jnp
from jax import lax
from jax.experimental import pallas as pl
from jax.experimental.pallas import tpu as pltpu
from jax.sharding import PartitionSpec as P

F32 = jnp.float32
BF16 = jnp.bfloat16
PARTS = 2


def kernel(
    sizes,
    text_len,
    ctrl_order,
    base_order,
    hid0,
    hid1,
    w0,
    w1,
    wo0,
    wo1,
    mod0,
    mod1,
    gain0,
    gain1,
    stale0,
    stale1,
    text0,
    text1,
    out0,
    out1,
    hbuf,
    wbuf,
    kvbuf,
    psend,
    pbuf,
    pair,
    hn,
    score_buf,
    blk_send,
    blk_buf,
    h_send,
    h_fwd,
    h_recv,
    w_send,
    w_recv,
    y_send,
    y_recv,
    kv_send,
    kv_recv,
    p_send,
    p_recv,
    pair_send,
    pair_recv,
    b_send,
    b_recv,
    load_sem,
    *held,
):
    n_groups, n_patch, n_sec, n_head = sizes
    n_sh = n_sec * n_head
    sources = (hid0, hid1, w0, w1, wo0, wo1, mod0, mod1, gain0, gain1, text0, text1)
    src_hids, src_ws = (hid0, hid1), (w0, w1)
    loads = [
        pltpu.make_async_copy(src, dst, load_sem.at[i])
        for i, (src, dst) in enumerate(zip(sources, held))
    ]
    for load in loads:
        load.start()
    hid0, hid1, w0, w1, wo0, wo1, mod0, mod1, gain0, gain1, text0, text1 = held
    hids, ws, wos = (hid0, hid1), (w0, w1), (wo0, wo1)
    mods, gains, stales, texts, outs = (
        (mod0, mod1),
        (gain0, gain1),
        (stale0, stale1),
        (text0, text1),
        (out0, out1),
    )
    rows, cols = hid0.shape
    head_size = stale0.shape[2]
    width = n_sh * cols
    blk = rows // n_patch
    g = lax.axis_index("groups")
    z = lax.axis_index("patch")
    x = lax.axis_index("section")
    c = lax.axis_index("head")
    me = x * n_head + c
    other = 1 - c

    def device(g_=None, z_=None, x_=None, c_=None):
        return (
            g if g_ is None else g_,
            z if z_ is None else z_,
            x if x_ is None else x_,
            c if c_ is None else c_,
        )

    def remote(src, dst, send, recv, dev):
        return pltpu.make_async_remote_copy(
            src_ref=src,
            dst_ref=dst,
            send_sem=send,
            recv_sem=recv,
            device_id=dev,
            device_id_type=pl.DeviceIdType.MESH,
        )

    def hid_copy(b, k):
        src = src_hids[b]
        if k == 0:
            dev = device(c_=other)
        else:
            dev = device(x_=lax.rem(x + k, n_sec))
        return remote(src, hbuf.at[b, me], h_send.at[b, k], h_recv.at[b, me], dev)

    def hid_start(b):
        for k in list(range(1, n_sec)) + [0]:
            hid_copy(b, k).start()

    def hid_fwd_copy(b, k):
        j = lax.rem(x + n_sec - k, n_sec) * n_head + c
        return remote(
            hbuf.at[b, j], hbuf.at[b, j], h_fwd.at[b, k], h_recv.at[b, j], device(c_=other)
        )

    def hid_forward(b):
        for k in range(1, n_sec):
            copy = hid_fwd_copy(b, k)
            copy.wait_recv()
            copy.start()

    def hid_wait(b):
        for k in range(n_sec):
            j = lax.rem(x + n_sec - k, n_sec) * n_head + other
            remote(
                hbuf.at[b, j], hbuf.at[b, j], h_fwd.at[b, 0], h_recv.at[b, j], device(c_=other)
            ).wait_recv()

    def w_copy(b, t, side):
        j = z - t if side == 0 else z + t
        src = src_ws[b].at[:, g] if t == 0 else wbuf.at[b, j, g]
        dev = device(z_=z + 1 if side == 0 else z - 1)
        return remote(src, wbuf.at[b, j, g], w_send.at[b, side, t], w_recv.at[b, j], dev)

    def kv_copy(b, t, side):
        j = z - t if side == 0 else z + t
        src = stales[b] if t == 0 else kvbuf.at[b, j]
        dev = device(z_=z + 1 if side == 0 else z - 1)
        return remote(src, kvbuf.at[b, j], kv_send.at[b, side, t], kv_recv.at[b, j], dev)

    def sends(t, side):
        if side == 0:
            return (z - t >= 0) & (z + 1 < n_patch)
        return (z + t < n_patch) & (z - 1 >= 0)

    def receives(t, side):
        return z - t - 1 >= 0 if side == 0 else z + t + 1 < n_patch

    def y_copy(b, j):
        return remote(
            wbuf.at[b, j, g], wbuf.at[b, j, g], y_send.at[b, j], y_recv.at[b, j], device(g_=1 - g)
        )

    def chain_start(make, b, t):
        for side in range(2):

            @pl.when(sends(t, side))
            def _():
                make(b, t, side).start()

    def w_arrive(b, t):
        for side in range(2):

            @pl.when(receives(t, side))
            def _():
                j = z - t - 1 if side == 0 else z + t + 1
                copy = remote(
                    wbuf.at[b, j, g],
                    wbuf.at[b, j, g],
                    y_send.at[b, j],
                    w_recv.at[b, j],
                    device(g_=1 - g),
                )
                copy.wait_recv()

        if t + 1 < n_patch - 1:
            chain_start(w_copy, b, t + 1)
        for side in range(2):

            @pl.when(receives(t, side))
            def _():
                y_copy(b, z - t - 1 if side == 0 else z + t + 1).start()

    def kv_arrive(b, t):
        for side in range(2):

            @pl.when(receives(t, side))
            def _():
                j = z - t - 1 if side == 0 else z + t + 1
                remote(
                    kvbuf.at[b, j],
                    kvbuf.at[b, j],
                    kv_send.at[b, side, 0],
                    kv_recv.at[b, j],
                    device(g_=1 - g),
                ).wait_recv()

        if t + 1 < n_patch - 1:
            chain_start(kv_copy, b, t + 1)

    def w_wait(b):
        for k in range(1, n_patch):
            j = lax.rem(z + k, n_patch)
            remote(
                wbuf.at[b, j, 1 - g],
                wbuf.at[b, j, 1 - g],
                y_send.at[b, j],
                y_recv.at[b, j],
                device(g_=1 - g),
            ).wait_recv()

    def mod_row(b, i, s):
        if len(mods[b].shape) == 3:
            return mods[b][i * n_sh + s]
        return mods[b][i : i + 1, pl.ds(pl.multiple_of(s * cols, cols), cols)]

    def normalize(b):
        step = min(32, rows)
        def body(i, carry):
            at = pl.ds(pl.multiple_of(i * step, step), step)
            total = jnp.zeros((step, 1), F32)
            for s in range(n_sh):
                total += jnp.sum(hbuf[b, s, at, :].astype(F32), axis=1, keepdims=True)
            center = total * (1.0 / width)
            spread = jnp.zeros((step, 1), F32)
            for s in range(n_sh):
                diff = hbuf[b, s, at, :].astype(F32) - center
                spread += jnp.sum(diff * diff, axis=1, keepdims=True)
            inv = lax.rsqrt(spread * (1.0 / width) + 1e-06)
            for s in range(n_sh):
                normed = (hbuf[b, s, at, :].astype(F32) - center) * inv
                hn[s, at, :] = (normed * (1.0 + mod_row(b, 1, s)) + mod_row(b, 0, s)).astype(BF16)
            return carry

        lax.fori_loop(0, rows // step, body, 0)

    def rms(values, gain):
        mean = jnp.mean(values * values, axis=-1, keepdims=True)
        return (values * lax.rsqrt(mean + 1e-06) * gain).astype(BF16)

    def project(b):
        half = ws[b].shape[2]

        def body(s, acc):
            for part in range(2):
                acc += jnp.dot(
                    hn[s, :, part * half : (part + 1) * half],
                    jnp.concatenate([wbuf[b, s, part, i] for i in range(3)], axis=1),
                    preferred_element_type=F32,
                )
            return acc

        qkv = lax.fori_loop(
            0, n_sh, body, jnp.zeros((rows, 3 * head_size), F32), unroll=n_sh <= 4
        )
        gain = gains[b]
        query = rms(qkv[:, :head_size], gain[0:1, :])
        kvbuf[b, z, 0] = rms(qkv[:, head_size : 2 * head_size], gain[1:2, :])
        kvbuf[b, z, 1] = qkv[:, 2 * head_size :].astype(BF16)
        return query

    def attend(b, query):
        scale = head_size ** (-0.5)
        text = texts[b]

        def scores(keys):
            return (
                lax.dot_general(query, keys, (((1,), (1,)), ((), ())), preferred_element_type=F32)
                * scale
            )

        slots = text.shape[1]
        text_score = scores(text[0])
        spot = lax.broadcasted_iota(jnp.int32, (query.shape[0], slots), 1)
        text_score = jnp.where(spot < text_len[0], text_score, -1e30)
        top = jnp.max(text_score, axis=1, keepdims=True)

        def first(s, top):
            score = scores(kvbuf[b, s, 0])
            score_buf[s] = score
            return jnp.maximum(top, jnp.max(score, axis=1, keepdims=True))

        top = lax.fori_loop(0, n_patch, first, top, unroll=n_patch <= 4)
        expo = jnp.exp(text_score - top)
        total = jnp.sum(expo, axis=1, keepdims=True)
        mixed = jnp.dot(expo.astype(BF16), text[1], preferred_element_type=F32)

        def second(s, carry):
            total, mixed = carry
            expo = jnp.exp(score_buf[s] - top)
            return (
                total + jnp.sum(expo, axis=1, keepdims=True),
                mixed + jnp.dot(expo.astype(BF16), kvbuf[b, s, 1], preferred_element_type=F32),
            )

        total, mixed = lax.fori_loop(
            0, n_patch, second, (total, mixed), unroll=n_patch <= 4
        )
        return (mixed / total).astype(BF16)

    piece = rows // PARTS

    def rows_of(r):
        return pl.ds(r * piece, piece)

    def section_of(k):
        return lax.rem(x + 1 + k, n_sec)

    def pair_copy(b, r, k):
        o = section_of(k)
        src = psend.at[b, o * n_head + other, rows_of(r)]
        dst = pair.at[b, o, rows_of(r)]
        return remote(src, dst, pair_send.at[b, r, o], pair_recv.at[b, r, o], device(c_=other))

    def p_copy(b, r, k):
        o = section_of(k)
        src = psend.at[b, o * n_head + c, rows_of(r)]
        dst = pbuf.at[b, x, rows_of(r)]
        return remote(src, dst, p_send.at[b, r, o], p_recv.at[b, r, x], device(x_=o))

    def out_part(b, attn, s):
        wo = wos[b]
        if len(wo.shape) == 3:
            weight = wo[s]
        else:
            weight = wo[:, pl.ds(pl.multiple_of(s * cols, cols), cols)]
        return jnp.dot(attn, weight, preferred_element_type=F32).astype(BF16)

    def out_start(b, r, attn):
        for k in range(n_sec):
            s = section_of(k) * n_head + other
            psend[b, s, rows_of(r), :] = out_part(b, attn, s)
            pair_copy(b, r, k).start()
        for k in range(n_sec - 1):
            o = section_of(k)
            mine = out_part(b, attn, o * n_head + c).astype(F32)
            pair_copy(b, r, k).wait_recv()
            total = mine + pair[b, o, rows_of(r), :].astype(F32)
            psend[b, o * n_head + c, rows_of(r), :] = total.astype(BF16)
            p_copy(b, r, k).start()
        pbuf[b, x, rows_of(r), :] = out_part(b, attn, me)

    def out_wait(b, r):
        pair_copy(b, r, n_sec - 1).wait_recv()
        for k in range(n_sec - 1):
            o = section_of(k)
            remote(
                pbuf.at[b, o, rows_of(r)],
                pbuf.at[b, o, rows_of(r)],
                p_send.at[b, r, o],
                p_recv.at[b, r, o],
                device(c_=other),
            ).wait_recv()

    def attend_out(b, query):
        for r in range(PARTS):
            out_start(b, r, attend(b, query[r * piece : (r + 1) * piece]))

    def gated(b, at):
        total = pair[b, x, at, :].astype(F32)
        for o in range(n_sec):
            total += pbuf[b, o, at, :].astype(F32)
        return hids[b][at, :].astype(F32) + mod_row(b, 2, me) * total

    def ctrl_finish():
        for d in range(n_patch):
            if d * PARTS % n_patch == 0:
                out_wait(0, d * PARTS // n_patch)
            at = pl.ds(d * blk, blk)
            out0[at, :] = gated(0, at).astype(BF16)

    def b_copy(k):
        d = lax.rem(z + k, n_patch)
        return remote(blk_send.at[d], blk_buf.at[z], b_send.at[d], b_recv.at[z], device(z_=d))

    def equal(one, two):
        return (one == two).astype(F32)

    def relay_start():
        def block_for(d):
            def outer(j, block):
                def inner(i, found):
                    return found + equal(base_order[d * n_patch + i], ctrl_order[z * n_patch + j])

                found = lax.fori_loop(0, n_patch, inner, jnp.float32(0.0))
                at = pl.ds(pl.multiple_of(j * blk, blk), blk)
                return block + found * out0[at, :].astype(F32)

            return lax.fori_loop(0, n_patch, outer, jnp.zeros((blk, cols), F32)).astype(BF16)

        for k in range(1, n_patch):
            d = lax.rem(z + k, n_patch)
            blk_send[d] = block_for(d)
            b_copy(k).start()
        blk_buf[z] = block_for(z)

    def relay_wait():
        for k in range(1, n_patch):
            d = lax.rem(z + k, n_patch)
            remote(
                blk_send.at[d], blk_buf.at[d], b_send.at[d], b_recv.at[d], device(z_=d)
            ).wait_recv()

    def base_finish():
        for i in range(n_patch):
            at = pl.ds(i * blk, blk)

            def outer(s, block):
                def inner(j, found):
                    return found + equal(ctrl_order[s * n_patch + j], base_order[z * n_patch + i])

                found = lax.fori_loop(0, n_patch, inner, jnp.float32(0.0))
                return block + found * blk_buf[s].astype(F32)

            relaid = lax.fori_loop(0, n_patch, outer, jnp.zeros((blk, cols), F32))
            if i * PARTS % n_patch == 0:
                out_wait(1, i * PARTS // n_patch)
            out1[at, :] = (gated(1, at) + relaid).astype(BF16)

    barrier = pltpu.get_barrier_semaphore()
    partners = [device(g_=1 - g)]
    partners += [device(z_=lax.rem(z + k, n_patch)) for k in range(1, n_patch)]
    partners += [device(x_=section_of(k)) for k in range(n_sec - 1)]
    partners.append(device(c_=other))
    for partner in partners:
        pl.semaphore_signal(
            barrier, inc=1, device_id=partner, device_id_type=pl.DeviceIdType.MESH
        )
    pl.semaphore_wait(barrier, len(partners))

    last = n_patch - 1
    chain_start(w_copy, 0, 0)
    hid_start(0)
    chain_start(kv_copy, 0, 0)
    hid_start(1)
    for load in loads:
        load.wait()
    for b in range(2):
        hbuf[b, me] = hids[b][...]
        for part in range(2):
            wbuf[b, z, part] = ws[b][:, part]
    hid_forward(0)
    w_arrive(0, 0)
    kv_arrive(0, 0)
    chain_start(w_copy, 1, 0)
    hid_wait(0)
    normalize(0)
    for t in range(1, last - 1):
        w_arrive(0, t)
        kv_arrive(0, t)
    hid_forward(1)
    w_arrive(1, 0)
    w_arrive(0, last - 1)
    w_wait(0)
    query = project(0)
    chain_start(kv_copy, 1, 0)
    for t in range(1, last - 1):
        w_arrive(1, t)
    kv_arrive(0, last - 1)
    attend_out(0, query)
    for t in range(last - 1):
        kv_arrive(1, t)
    hid_wait(1)
    normalize(1)
    w_arrive(1, last - 1)
    ctrl_finish()
    relay_start()
    w_wait(1)
    query = project(1)
    kv_arrive(1, last - 1)
    attend_out(1, query)
    relay_wait()
    base_finish()

    for b in range(2):
        for k in range(n_sec):
            hid_copy(b, k).wait_send()
        for k in range(1, n_sec):
            hid_fwd_copy(b, k).wait_send()
        for t in range(last):
            for side in range(2):

                @pl.when(sends(t, side))
                def _():
                    w_copy(b, t, side).wait_send()
                    kv_copy(b, t, side).wait_send()

        for k in range(1, n_patch):
            y_copy(b, lax.rem(z + k, n_patch)).wait_send()
        for k in range(n_sec - 1):
            for r in range(PARTS):
                p_copy(b, r, k).wait_send()
        for k in range(n_sec):
            for r in range(PARTS):
                pair_copy(b, r, k).wait_send()
    for k in range(1, n_patch):
        b_copy(k).wait_send()


def local(
    sizes,
    ctrl_hidden,
    base_hidden,
    ctrl_qkv_weight,
    base_qkv_weight,
    ctrl_out_weight,
    base_out_weight,
    ctrl_mod,
    base_mod,
    ctrl_qk_gain,
    base_qk_gain,
    ctrl_stale,
    base_stale,
    ctrl_text,
    base_text,
    ctrl_order,
    base_order,
    text_len,
):
    n_groups, n_patch, n_sec, n_head = sizes
    n_sh = n_sec * n_head
    rows, cols = ctrl_hidden.shape
    w_rows, _, head_size = ctrl_qkv_weight.shape
    blk = rows // n_patch

    def halves(weight):
        return weight.transpose(1, 0, 2).reshape(3, 2, w_rows // 2, head_size)

    def by_columns(weight):
        if cols % 128 == 0:
            return weight
        return weight.reshape(weight.shape[0], n_sh, cols).transpose(1, 0, 2)

    def mod_rows(mod):
        return mod if cols % 128 == 0 else mod.reshape(3 * n_sh, 1, cols)

    operands = (
        ctrl_hidden,
        base_hidden,
        halves(ctrl_qkv_weight),
        halves(base_qkv_weight),
        by_columns(ctrl_out_weight),
        by_columns(base_out_weight),
        mod_rows(ctrl_mod),
        mod_rows(base_mod),
        ctrl_qk_gain,
        base_qk_gain,
        ctrl_stale,
        base_stale,
        ctrl_text,
        base_text,
    )
    held = operands[:10] + operands[12:]
    smem = pl.BlockSpec(memory_space=pltpu.SMEM)
    vmem = pl.BlockSpec(memory_space=pltpu.VMEM)
    hbm = pl.BlockSpec(memory_space=pltpu.HBM)
    dma = pltpu.SemaphoreType.DMA
    out = jax.ShapeDtypeStruct((rows, cols), BF16)
    return pl.pallas_call(
        functools.partial(kernel, sizes),
        out_shape=(out, out),
        in_specs=[smem] * 3 + [hbm] * 14,
        out_specs=(vmem, vmem),
        scratch_shapes=[
            pltpu.VMEM((2, n_sh, rows, cols), BF16),
            pltpu.VMEM((2, n_patch, 2, 3, w_rows // 2, head_size), BF16),
            pltpu.VMEM((2, n_patch, 2, rows, head_size), BF16),
            pltpu.VMEM((2, n_sh, rows, cols), BF16),
            pltpu.VMEM((2, n_sec, rows, cols), BF16),
            pltpu.VMEM((2, n_sec, rows, cols), BF16),
            pltpu.VMEM((n_sh, rows, cols), BF16),
            pltpu.VMEM((n_patch, rows // PARTS, rows), F32),
            pltpu.VMEM((n_patch, blk, cols), BF16),
            pltpu.VMEM((n_patch, blk, cols), BF16),
            dma((2, n_sec)),
            dma((2, n_sec)),
            dma((2, n_sh)),
            dma((2, 2, n_patch)),
            dma((2, n_patch)),
            dma((2, n_patch)),
            dma((2, n_patch)),
            dma((2, 2, n_patch)),
            dma((2, n_patch)),
            dma((2, PARTS, n_sec)),
            dma((2, PARTS, n_sec)),
            dma((2, PARTS, n_sec)),
            dma((2, PARTS, n_sec)),
            dma((n_patch,)),
            dma((n_patch,)),
            dma((len(held),)),
        ]
        + [pltpu.VMEM(array.shape, array.dtype) for array in held],
        compiler_params=pltpu.CompilerParams(
            collective_id=0, has_side_effects=True, vmem_limit_bytes=56 * 1024 * 1024
        ),
    )(
        text_len,
        ctrl_order,
        base_order,
        *operands,
    )


def solution(mesh):
    sizes = tuple(mesh.shape[name] for name in ("groups", "patch", "section", "head"))
    in_specs = (
        P(("groups", "patch"), ("section", "head")),
        P(("groups", "patch"), ("section", "head")),
        P("patch", None, ("section", "head")),
        P("patch", None, ("section", "head")),
        P(("section", "head"), None),
        P(("section", "head"), None),
        P(),
        P(),
        P(),
        P(),
        P(None, ("groups", "patch"), ("section", "head")),
        P(None, ("groups", "patch"), ("section", "head")),
        P(None, "groups", ("section", "head")),
        P(None, "groups", ("section", "head")),
        P(),
        P(),
        P("groups"),
    )
    out_specs = (
        P(("groups", "patch"), ("section", "head")),
        P(("groups", "patch"), ("section", "head")),
    )
    return jax.shard_map(
        functools.partial(local, sizes),
        mesh=mesh,
        in_specs=in_specs,
        out_specs=out_specs,
        check_vma=False,
    )
```

```python
import functools

import jax
import jax.numpy as jnp
from jax import lax
from jax.experimental import pallas as pl
from jax.experimental.pallas import tpu as pltpu
from jax.sharding import PartitionSpec as P

F32 = jnp.float32
BF16 = jnp.bfloat16
PARTS = 2


def kernel(
    sizes,
    text_len,
    ctrl_order,
    base_order,
    hid0,
    hid1,
    w0,
    w1,
    wo0,
    wo1,
    mod0,
    mod1,
    gain0,
    gain1,
    stale0,
    stale1,
    text0,
    text1,
    out0,
    out1,
    hbuf,
    wbuf,
    kvbuf,
    psend,
    pbuf,
    pair,
    hn,
    score_buf,
    blk_send,
    blk_buf,
    h_send,
    h_fwd,
    h_recv,
    w_send,
    w_recv,
    y_send,
    y_recv,
    kv_send,
    kv_recv,
    p_send,
    p_recv,
    pair_send,
    pair_recv,
    b_send,
    b_recv,
    load_sem,
    *held,
):
    n_groups, n_patch, n_sec, n_head = sizes
    n_sh = n_sec * n_head
    sources = (hid0, hid1, w0, w1, wo0, wo1, mod0, mod1, gain0, gain1, text0, text1)
    src_hids, src_ws = (hid0, hid1), (w0, w1)
    loads = [
        pltpu.make_async_copy(src, dst, load_sem.at[i])
        for i, (src, dst) in enumerate(zip(sources, held))
    ]
    for load in loads:
        load.start()
    hid0, hid1, w0, w1, wo0, wo1, mod0, mod1, gain0, gain1, text0, text1 = held
    hids, ws, wos = (hid0, hid1), (w0, w1), (wo0, wo1)
    mods, gains, stales, texts, outs = (
        (mod0, mod1),
        (gain0, gain1),
        (stale0, stale1),
        (text0, text1),
        (out0, out1),
    )
    rows, cols = hid0.shape
    head_size = stale0.shape[2]
    width = n_sh * cols
    blk = rows // n_patch
    g = lax.axis_index("groups")
    z = lax.axis_index("patch")
    x = lax.axis_index("section")
    c = lax.axis_index("head")
    me = x * n_head + c
    other = 1 - c

    def device(g_=None, z_=None, x_=None, c_=None):
        return (
            g if g_ is None else g_,
            z if z_ is None else z_,
            x if x_ is None else x_,
            c if c_ is None else c_,
        )

    def remote(src, dst, send, recv, dev):
        return pltpu.make_async_remote_copy(
            src_ref=src,
            dst_ref=dst,
            send_sem=send,
            recv_sem=recv,
            device_id=dev,
            device_id_type=pl.DeviceIdType.MESH,
        )

    def hid_copy(b, k):
        src = src_hids[b]
        if k == 0:
            dev = device(c_=other)
        else:
            dev = device(x_=lax.rem(x + k, n_sec))
        return remote(src, hbuf.at[b, me], h_send.at[b, k], h_recv.at[b, me], dev)

    def hid_start(b):
        for k in list(range(1, n_sec)) + [0]:
            hid_copy(b, k).start()

    def hid_fwd_copy(b, k):
        j = lax.rem(x + n_sec - k, n_sec) * n_head + c
        return remote(
            hbuf.at[b, j], hbuf.at[b, j], h_fwd.at[b, k], h_recv.at[b, j], device(c_=other)
        )

    def hid_forward(b):
        for k in range(1, n_sec):
            copy = hid_fwd_copy(b, k)
            copy.wait_recv()
            copy.start()

    def hid_wait(b):
        for k in range(n_sec):
            j = lax.rem(x + n_sec - k, n_sec) * n_head + other
            remote(
                hbuf.at[b, j], hbuf.at[b, j], h_fwd.at[b, 0], h_recv.at[b, j], device(c_=other)
            ).wait_recv()

    def w_copy(b, t, side):
        j = z - t if side == 0 else z + t
        src = src_ws[b].at[:, g] if t == 0 else wbuf.at[b, j, g]
        dev = device(z_=z + 1 if side == 0 else z - 1)
        return remote(src, wbuf.at[b, j, g], w_send.at[b, side, t], w_recv.at[b, j], dev)

    def kv_copy(b, t, side):
        j = z - t if side == 0 else z + t
        src = stales[b] if t == 0 else kvbuf.at[b, j]
        dev = device(z_=z + 1 if side == 0 else z - 1)
        return remote(src, kvbuf.at[b, j], kv_send.at[b, side, t], kv_recv.at[b, j], dev)

    def sends(t, side):
        if side == 0:
            return (z - t >= 0) & (z + 1 < n_patch)
        return (z + t < n_patch) & (z - 1 >= 0)

    def receives(t, side):
        return z - t - 1 >= 0 if side == 0 else z + t + 1 < n_patch

    def y_copy(b, j):
        return remote(
            wbuf.at[b, j, g], wbuf.at[b, j, g], y_send.at[b, j], y_recv.at[b, j], device(g_=1 - g)
        )

    def chain_start(make, b, t):
        for side in range(2):

            @pl.when(sends(t, side))
            def _():
                make(b, t, side).start()

    def w_arrive(b, t):
        for side in range(2):

            @pl.when(receives(t, side))
            def _():
                j = z - t - 1 if side == 0 else z + t + 1
                copy = remote(
                    wbuf.at[b, j, g],
                    wbuf.at[b, j, g],
                    y_send.at[b, j],
                    w_recv.at[b, j],
                    device(g_=1 - g),
                )
                copy.wait_recv()

        if t + 1 < n_patch - 1:
            chain_start(w_copy, b, t + 1)
        for side in range(2):

            @pl.when(receives(t, side))
            def _():
                y_copy(b, z - t - 1 if side == 0 else z + t + 1).start()

    def kv_arrive(b, t):
        for side in range(2):

            @pl.when(receives(t, side))
            def _():
                j = z - t - 1 if side == 0 else z + t + 1
                remote(
                    kvbuf.at[b, j],
                    kvbuf.at[b, j],
                    kv_send.at[b, side, 0],
                    kv_recv.at[b, j],
                    device(g_=1 - g),
                ).wait_recv()

        if t + 1 < n_patch - 1:
            chain_start(kv_copy, b, t + 1)

    def w_wait(b):
        for k in range(1, n_patch):
            j = lax.rem(z + k, n_patch)
            remote(
                wbuf.at[b, j, 1 - g],
                wbuf.at[b, j, 1 - g],
                y_send.at[b, j],
                y_recv.at[b, j],
                device(g_=1 - g),
            ).wait_recv()

    def mod_row(b, i, s):
        if len(mods[b].shape) == 3:
            return mods[b][i * n_sh + s]
        return mods[b][i : i + 1, pl.ds(pl.multiple_of(s * cols, cols), cols)]

    def normalize(b):
        step = min(32, rows)
        def body(i, carry):
            at = pl.ds(pl.multiple_of(i * step, step), step)
            total = jnp.zeros((step, 1), F32)
            for s in range(n_sh):
                total += jnp.sum(hbuf[b, s, at, :].astype(F32), axis=1, keepdims=True)
            center = total * (1.0 / width)
            spread = jnp.zeros((step, 1), F32)
            for s in range(n_sh):
                diff = hbuf[b, s, at, :].astype(F32) - center
                spread += jnp.sum(diff * diff, axis=1, keepdims=True)
            inv = lax.rsqrt(spread * (1.0 / width) + 1e-06)
            for s in range(n_sh):
                normed = (hbuf[b, s, at, :].astype(F32) - center) * inv
                hn[s, at, :] = (normed * (1.0 + mod_row(b, 1, s)) + mod_row(b, 0, s)).astype(BF16)
            return carry

        lax.fori_loop(0, rows // step, body, 0)

    def rms(values, gain):
        mean = jnp.mean(values * values, axis=-1, keepdims=True)
        return (values * lax.rsqrt(mean + 1e-06) * gain).astype(BF16)

    def project(b):
        half = ws[b].shape[2]

        def body(s, acc):
            for part in range(2):
                acc += jnp.dot(
                    hn[s, :, part * half : (part + 1) * half],
                    jnp.concatenate([wbuf[b, s, part, i] for i in range(3)], axis=1),
                    preferred_element_type=F32,
                )
            return acc

        qkv = lax.fori_loop(
            0, n_sh, body, jnp.zeros((rows, 3 * head_size), F32), unroll=n_sh <= 4
        )
        gain = gains[b]
        query = rms(qkv[:, :head_size], gain[0:1, :])
        kvbuf[b, z, 0] = rms(qkv[:, head_size : 2 * head_size], gain[1:2, :])
        kvbuf[b, z, 1] = qkv[:, 2 * head_size :].astype(BF16)
        return query

    def attend(b, query):
        scale = head_size ** (-0.5)
        text = texts[b]

        def scores(keys):
            return (
                lax.dot_general(query, keys, (((1,), (1,)), ((), ())), preferred_element_type=F32)
                * scale
            )

        slots = text.shape[1]
        text_score = scores(text[0])
        spot = lax.broadcasted_iota(jnp.int32, (query.shape[0], slots), 1)
        text_score = jnp.where(spot < text_len[0], text_score, -1e30)
        top = jnp.max(text_score, axis=1, keepdims=True)

        def first(s, top):
            score = scores(kvbuf[b, s, 0])
            score_buf[s] = score
            return jnp.maximum(top, jnp.max(score, axis=1, keepdims=True))

        top = lax.fori_loop(0, n_patch, first, top, unroll=n_patch <= 4)
        expo = jnp.exp(text_score - top)
        total = jnp.sum(expo, axis=1, keepdims=True)
        mixed = jnp.dot(expo.astype(BF16), text[1], preferred_element_type=F32)

        def second(s, carry):
            total, mixed = carry
            expo = jnp.exp(score_buf[s] - top)
            return (
                total + jnp.sum(expo, axis=1, keepdims=True),
                mixed + jnp.dot(expo.astype(BF16), kvbuf[b, s, 1], preferred_element_type=F32),
            )

        total, mixed = lax.fori_loop(
            0, n_patch, second, (total, mixed), unroll=n_patch <= 4
        )
        return (mixed / total).astype(BF16)

    piece = rows // PARTS

    def rows_of(r):
        return pl.ds(r * piece, piece)

    def section_of(k):
        return lax.rem(x + 1 + k, n_sec)

    def pair_copy(b, r, k):
        o = section_of(k)
        src = psend.at[b, o * n_head + other, rows_of(r)]
        dst = pair.at[b, o, rows_of(r)]
        return remote(src, dst, pair_send.at[b, r, o], pair_recv.at[b, r, o], device(c_=other))

    def p_copy(b, r, k):
        o = section_of(k)
        src = psend.at[b, o * n_head + c, rows_of(r)]
        dst = pbuf.at[b, x, rows_of(r)]
        return remote(src, dst, p_send.at[b, r, o], p_recv.at[b, r, x], device(x_=o))

    def out_part(b, attn, s):
        wo = wos[b]
        if len(wo.shape) == 3:
            weight = wo[s]
        else:
            weight = wo[:, pl.ds(pl.multiple_of(s * cols, cols), cols)]
        return jnp.dot(attn, weight, preferred_element_type=F32).astype(BF16)

    def out_start(b, r, attn):
        for k in range(n_sec):
            s = section_of(k) * n_head + other
            psend[b, s, rows_of(r), :] = out_part(b, attn, s)
            pair_copy(b, r, k).start()
        for k in range(n_sec - 1):
            o = section_of(k)
            mine = out_part(b, attn, o * n_head + c).astype(F32)
            pair_copy(b, r, k).wait_recv()
            total = mine + pair[b, o, rows_of(r), :].astype(F32)
            psend[b, o * n_head + c, rows_of(r), :] = total.astype(BF16)
            p_copy(b, r, k).start()
        pbuf[b, x, rows_of(r), :] = out_part(b, attn, me)

    def out_wait(b, r):
        pair_copy(b, r, n_sec - 1).wait_recv()
        for k in range(n_sec - 1):
            o = section_of(k)
            remote(
                pbuf.at[b, o, rows_of(r)],
                pbuf.at[b, o, rows_of(r)],
                p_send.at[b, r, o],
                p_recv.at[b, r, o],
                device(c_=other),
            ).wait_recv()

    def attend_out(b, query):
        for r in range(PARTS):
            out_start(b, r, attend(b, query[r * piece : (r + 1) * piece]))

    def gated(b, at):
        total = pair[b, x, at, :].astype(F32)
        for o in range(n_sec):
            total += pbuf[b, o, at, :].astype(F32)
        return hids[b][at, :].astype(F32) + mod_row(b, 2, me) * total

    def ctrl_finish():
        for d in range(n_patch):
            if d * PARTS % n_patch == 0:
                out_wait(0, d * PARTS // n_patch)
            at = pl.ds(d * blk, blk)
            out0[at, :] = gated(0, at).astype(BF16)

    def b_copy(k):
        d = lax.rem(z + k, n_patch)
        return remote(blk_send.at[d], blk_buf.at[z], b_send.at[d], b_recv.at[z], device(z_=d))

    def equal(one, two):
        return (one == two).astype(F32)

    def relay_start():
        def block_for(d):
            def outer(j, block):
                def inner(i, found):
                    return found + equal(base_order[d * n_patch + i], ctrl_order[z * n_patch + j])

                found = lax.fori_loop(0, n_patch, inner, jnp.float32(0.0))
                at = pl.ds(pl.multiple_of(j * blk, blk), blk)
                return block + found * out0[at, :].astype(F32)

            return lax.fori_loop(0, n_patch, outer, jnp.zeros((blk, cols), F32)).astype(BF16)

        for k in range(1, n_patch):
            d = lax.rem(z + k, n_patch)
            blk_send[d] = block_for(d)
            b_copy(k).start()
        blk_buf[z] = block_for(z)

    def relay_wait():
        for k in range(1, n_patch):
            d = lax.rem(z + k, n_patch)
            remote(
                blk_send.at[d], blk_buf.at[d], b_send.at[d], b_recv.at[d], device(z_=d)
            ).wait_recv()

    def base_finish():
        for i in range(n_patch):
            at = pl.ds(i * blk, blk)

            def outer(s, block):
                def inner(j, found):
                    return found + equal(ctrl_order[s * n_patch + j], base_order[z * n_patch + i])

                found = lax.fori_loop(0, n_patch, inner, jnp.float32(0.0))
                return block + found * blk_buf[s].astype(F32)

            relaid = lax.fori_loop(0, n_patch, outer, jnp.zeros((blk, cols), F32))
            if i * PARTS % n_patch == 0:
                out_wait(1, i * PARTS // n_patch)
            out1[at, :] = (gated(1, at) + relaid).astype(BF16)

    barrier = pltpu.get_barrier_semaphore()
    partners = [device(g_=1 - g)]
    partners += [device(z_=lax.rem(z + k, n_patch)) for k in range(1, n_patch)]
    partners += [device(x_=section_of(k)) for k in range(n_sec - 1)]
    partners.append(device(c_=other))
    for partner in partners:
        pl.semaphore_signal(
            barrier, inc=1, device_id=partner, device_id_type=pl.DeviceIdType.MESH
        )
    pl.semaphore_wait(barrier, len(partners))

    last = n_patch - 1
    chain_start(w_copy, 0, 0)
    hid_start(0)
    chain_start(kv_copy, 0, 0)
    chain_start(w_copy, 1, 0)
    hid_start(1)
    for load in loads:
        load.wait()
    for b in range(2):
        hbuf[b, me] = hids[b][...]
        for part in range(2):
            wbuf[b, z, part] = ws[b][:, part]
    hid_forward(0)
    w_arrive(0, 0)
    kv_arrive(0, 0)
    for t in range(1, last - 1):
        w_arrive(0, t)
        kv_arrive(0, t)
    hid_forward(1)
    w_arrive(1, 0)
    hid_wait(0)
    normalize(0)
    w_arrive(0, last - 1)
    w_wait(0)
    query = project(0)
    chain_start(kv_copy, 1, 0)
    for t in range(1, last - 1):
        w_arrive(1, t)
    kv_arrive(0, last - 1)
    attend_out(0, query)
    for t in range(last - 1):
        kv_arrive(1, t)
    hid_wait(1)
    normalize(1)
    w_arrive(1, last - 1)
    ctrl_finish()
    relay_start()
    w_wait(1)
    query = project(1)
    kv_arrive(1, last - 1)
    attend_out(1, query)
    relay_wait()
    base_finish()

    for b in range(2):
        for k in range(n_sec):
            hid_copy(b, k).wait_send()
        for k in range(1, n_sec):
            hid_fwd_copy(b, k).wait_send()
        for t in range(last):
            for side in range(2):

                @pl.when(sends(t, side))
                def _():
                    w_copy(b, t, side).wait_send()
                    kv_copy(b, t, side).wait_send()

        for k in range(1, n_patch):
            y_copy(b, lax.rem(z + k, n_patch)).wait_send()
        for k in range(n_sec - 1):
            for r in range(PARTS):
                p_copy(b, r, k).wait_send()
        for k in range(n_sec):
            for r in range(PARTS):
                pair_copy(b, r, k).wait_send()
    for k in range(1, n_patch):
        b_copy(k).wait_send()


def local(
    sizes,
    ctrl_hidden,
    base_hidden,
    ctrl_qkv_weight,
    base_qkv_weight,
    ctrl_out_weight,
    base_out_weight,
    ctrl_mod,
    base_mod,
    ctrl_qk_gain,
    base_qk_gain,
    ctrl_stale,
    base_stale,
    ctrl_text,
    base_text,
    ctrl_order,
    base_order,
    text_len,
):
    n_groups, n_patch, n_sec, n_head = sizes
    n_sh = n_sec * n_head
    rows, cols = ctrl_hidden.shape
    w_rows, _, head_size = ctrl_qkv_weight.shape
    blk = rows // n_patch

    def halves(weight):
        return weight.transpose(1, 0, 2).reshape(3, 2, w_rows // 2, head_size)

    def by_columns(weight):
        if cols % 128 == 0:
            return weight
        return weight.reshape(weight.shape[0], n_sh, cols).transpose(1, 0, 2)

    def mod_rows(mod):
        return mod if cols % 128 == 0 else mod.reshape(3 * n_sh, 1, cols)

    operands = (
        ctrl_hidden,
        base_hidden,
        halves(ctrl_qkv_weight),
        halves(base_qkv_weight),
        by_columns(ctrl_out_weight),
        by_columns(base_out_weight),
        mod_rows(ctrl_mod),
        mod_rows(base_mod),
        ctrl_qk_gain,
        base_qk_gain,
        ctrl_stale,
        base_stale,
        ctrl_text,
        base_text,
    )
    held = operands[:10] + operands[12:]
    smem = pl.BlockSpec(memory_space=pltpu.SMEM)
    vmem = pl.BlockSpec(memory_space=pltpu.VMEM)
    hbm = pl.BlockSpec(memory_space=pltpu.HBM)
    dma = pltpu.SemaphoreType.DMA
    out = jax.ShapeDtypeStruct((rows, cols), BF16)
    return pl.pallas_call(
        functools.partial(kernel, sizes),
        out_shape=(out, out),
        in_specs=[smem] * 3 + [hbm] * 14,
        out_specs=(vmem, vmem),
        scratch_shapes=[
            pltpu.VMEM((2, n_sh, rows, cols), BF16),
            pltpu.VMEM((2, n_patch, 2, 3, w_rows // 2, head_size), BF16),
            pltpu.VMEM((2, n_patch, 2, rows, head_size), BF16),
            pltpu.VMEM((2, n_sh, rows, cols), BF16),
            pltpu.VMEM((2, n_sec, rows, cols), BF16),
            pltpu.VMEM((2, n_sec, rows, cols), BF16),
            pltpu.VMEM((n_sh, rows, cols), BF16),
            pltpu.VMEM((n_patch, rows // PARTS, rows), F32),
            pltpu.VMEM((n_patch, blk, cols), BF16),
            pltpu.VMEM((n_patch, blk, cols), BF16),
            dma((2, n_sec)),
            dma((2, n_sec)),
            dma((2, n_sh)),
            dma((2, 2, n_patch)),
            dma((2, n_patch)),
            dma((2, n_patch)),
            dma((2, n_patch)),
            dma((2, 2, n_patch)),
            dma((2, n_patch)),
            dma((2, PARTS, n_sec)),
            dma((2, PARTS, n_sec)),
            dma((2, PARTS, n_sec)),
            dma((2, PARTS, n_sec)),
            dma((n_patch,)),
            dma((n_patch,)),
            dma((len(held),)),
        ]
        + [pltpu.VMEM(array.shape, array.dtype) for array in held],
        compiler_params=pltpu.CompilerParams(
            collective_id=0, has_side_effects=True, vmem_limit_bytes=56 * 1024 * 1024
        ),
    )(
        text_len,
        ctrl_order,
        base_order,
        *operands,
    )


def solution(mesh):
    sizes = tuple(mesh.shape[name] for name in ("groups", "patch", "section", "head"))
    in_specs = (
        P(("groups", "patch"), ("section", "head")),
        P(("groups", "patch"), ("section", "head")),
        P("patch", None, ("section", "head")),
        P("patch", None, ("section", "head")),
        P(("section", "head"), None),
        P(("section", "head"), None),
        P(),
        P(),
        P(),
        P(),
        P(None, ("groups", "patch"), ("section", "head")),
        P(None, ("groups", "patch"), ("section", "head")),
        P(None, "groups", ("section", "head")),
        P(None, "groups", ("section", "head")),
        P(),
        P(),
        P("groups"),
    )
    out_specs = (
        P(("groups", "patch"), ("section", "head")),
        P(("groups", "patch"), ("section", "head")),
    )
    return jax.shard_map(
        functools.partial(local, sizes),
        mesh=mesh,
        in_specs=in_specs,
        out_specs=out_specs,
        check_vma=False,
    )
```

```python
import functools

import jax
import jax.numpy as jnp
from jax import lax
from jax.experimental import pallas as pl
from jax.experimental.pallas import tpu as pltpu
from jax.sharding import PartitionSpec as P

F32 = jnp.float32
BF16 = jnp.bfloat16
PARTS = 2


def kernel(
    sizes,
    text_len,
    ctrl_order,
    base_order,
    hid0,
    hid1,
    w0,
    w1,
    wo0,
    wo1,
    mod0,
    mod1,
    gain0,
    gain1,
    stale0,
    stale1,
    text0,
    text1,
    out0,
    out1,
    hbuf,
    wbuf,
    kvbuf,
    psend,
    pbuf,
    pair,
    hn,
    score_buf,
    blk_send,
    blk_buf,
    h_send,
    h_fwd,
    h_recv,
    w_send,
    w_recv,
    y_send,
    y_recv,
    kv_send,
    kv_recv,
    p_send,
    p_recv,
    pair_send,
    pair_recv,
    b_send,
    b_recv,
    load_sem,
    *held,
):
    n_groups, n_patch, n_sec, n_head = sizes
    n_sh = n_sec * n_head
    sources = (hid0, hid1, w0, w1, wo0, wo1, mod0, mod1, gain0, gain1, text0, text1)
    src_hids, src_ws = (hid0, hid1), (w0, w1)
    loads = [
        pltpu.make_async_copy(src, dst, load_sem.at[i])
        for i, (src, dst) in enumerate(zip(sources, held))
    ]
    for load in loads:
        load.start()
    hid0, hid1, w0, w1, wo0, wo1, mod0, mod1, gain0, gain1, text0, text1 = held
    hids, ws, wos = (hid0, hid1), (w0, w1), (wo0, wo1)
    mods, gains, stales, texts, outs = (
        (mod0, mod1),
        (gain0, gain1),
        (stale0, stale1),
        (text0, text1),
        (out0, out1),
    )
    rows, cols = hid0.shape
    head_size = stale0.shape[2]
    width = n_sh * cols
    blk = rows // n_patch
    g = lax.axis_index("groups")
    z = lax.axis_index("patch")
    x = lax.axis_index("section")
    c = lax.axis_index("head")
    me = x * n_head + c
    other = 1 - c

    def device(g_=None, z_=None, x_=None, c_=None):
        return (
            g if g_ is None else g_,
            z if z_ is None else z_,
            x if x_ is None else x_,
            c if c_ is None else c_,
        )

    def remote(src, dst, send, recv, dev):
        return pltpu.make_async_remote_copy(
            src_ref=src,
            dst_ref=dst,
            send_sem=send,
            recv_sem=recv,
            device_id=dev,
            device_id_type=pl.DeviceIdType.MESH,
        )

    def hid_copy(b, k):
        src = src_hids[b]
        if k == 0:
            dev = device(c_=other)
        else:
            dev = device(x_=lax.rem(x + k, n_sec))
        return remote(src, hbuf.at[b, me], h_send.at[b, k], h_recv.at[b, me], dev)

    def hid_start(b):
        for k in list(range(1, n_sec)) + [0]:
            hid_copy(b, k).start()

    def hid_fwd_copy(b, k):
        j = lax.rem(x + n_sec - k, n_sec) * n_head + c
        return remote(
            hbuf.at[b, j], hbuf.at[b, j], h_fwd.at[b, k], h_recv.at[b, j], device(c_=other)
        )

    def hid_forward(b):
        for k in range(1, n_sec):
            copy = hid_fwd_copy(b, k)
            copy.wait_recv()
            copy.start()

    def hid_wait(b):
        for k in range(n_sec):
            j = lax.rem(x + n_sec - k, n_sec) * n_head + other
            remote(
                hbuf.at[b, j], hbuf.at[b, j], h_fwd.at[b, 0], h_recv.at[b, j], device(c_=other)
            ).wait_recv()

    def w_copy(b, t, side):
        j = z - t if side == 0 else z + t
        src = src_ws[b].at[:, g] if t == 0 else wbuf.at[b, j, g]
        dev = device(z_=z + 1 if side == 0 else z - 1)
        return remote(src, wbuf.at[b, j, g], w_send.at[b, side, t], w_recv.at[b, j], dev)

    def kv_copy(b, t, side):
        j = z - t if side == 0 else z + t
        src = stales[b] if t == 0 else kvbuf.at[b, j]
        dev = device(z_=z + 1 if side == 0 else z - 1)
        return remote(src, kvbuf.at[b, j], kv_send.at[b, side, t], kv_recv.at[b, j], dev)

    def sends(t, side):
        if side == 0:
            return (z - t >= 0) & (z + 1 < n_patch)
        return (z + t < n_patch) & (z - 1 >= 0)

    def receives(t, side):
        return z - t - 1 >= 0 if side == 0 else z + t + 1 < n_patch

    def y_copy(b, j):
        return remote(
            wbuf.at[b, j, g], wbuf.at[b, j, g], y_send.at[b, j], y_recv.at[b, j], device(g_=1 - g)
        )

    def chain_start(make, b, t):
        for side in range(2):

            @pl.when(sends(t, side))
            def _():
                make(b, t, side).start()

    def w_arrive(b, t):
        for side in range(2):

            @pl.when(receives(t, side))
            def _():
                j = z - t - 1 if side == 0 else z + t + 1
                copy = remote(
                    wbuf.at[b, j, g],
                    wbuf.at[b, j, g],
                    y_send.at[b, j],
                    w_recv.at[b, j],
                    device(g_=1 - g),
                )
                copy.wait_recv()

        if t + 1 < n_patch - 1:
            chain_start(w_copy, b, t + 1)
        for side in range(2):

            @pl.when(receives(t, side))
            def _():
                y_copy(b, z - t - 1 if side == 0 else z + t + 1).start()

    def kv_arrive(b, t):
        for side in range(2):

            @pl.when(receives(t, side))
            def _():
                j = z - t - 1 if side == 0 else z + t + 1
                remote(
                    kvbuf.at[b, j],
                    kvbuf.at[b, j],
                    kv_send.at[b, side, 0],
                    kv_recv.at[b, j],
                    device(g_=1 - g),
                ).wait_recv()

        if t + 1 < n_patch - 1:
            chain_start(kv_copy, b, t + 1)

    def w_wait(b):
        for k in range(1, n_patch):
            j = lax.rem(z + k, n_patch)
            remote(
                wbuf.at[b, j, 1 - g],
                wbuf.at[b, j, 1 - g],
                y_send.at[b, j],
                y_recv.at[b, j],
                device(g_=1 - g),
            ).wait_recv()

    def mod_row(b, i, s):
        if len(mods[b].shape) == 3:
            return mods[b][i * n_sh + s]
        return mods[b][i : i + 1, pl.ds(pl.multiple_of(s * cols, cols), cols)]

    def normalize(b):
        step = min(32, rows)
        def body(i, carry):
            at = pl.ds(pl.multiple_of(i * step, step), step)
            total = jnp.zeros((step, 1), F32)
            for s in range(n_sh):
                total += jnp.sum(hbuf[b, s, at, :].astype(F32), axis=1, keepdims=True)
            center = total * (1.0 / width)
            spread = jnp.zeros((step, 1), F32)
            for s in range(n_sh):
                diff = hbuf[b, s, at, :].astype(F32) - center
                spread += jnp.sum(diff * diff, axis=1, keepdims=True)
            inv = lax.rsqrt(spread * (1.0 / width) + 1e-06)
            for s in range(n_sh):
                normed = (hbuf[b, s, at, :].astype(F32) - center) * inv
                hn[s, at, :] = (normed * (1.0 + mod_row(b, 1, s)) + mod_row(b, 0, s)).astype(BF16)
            return carry

        lax.fori_loop(0, rows // step, body, 0)

    def rms(values, gain):
        mean = jnp.mean(values * values, axis=-1, keepdims=True)
        return (values * lax.rsqrt(mean + 1e-06) * gain).astype(BF16)

    def project(b):
        half = ws[b].shape[2]

        def body(s, acc):
            for part in range(2):
                acc += jnp.dot(
                    hn[s, :, part * half : (part + 1) * half],
                    jnp.concatenate([wbuf[b, s, part, i] for i in range(3)], axis=1),
                    preferred_element_type=F32,
                )
            return acc

        qkv = lax.fori_loop(
            0, n_sh, body, jnp.zeros((rows, 3 * head_size), F32), unroll=n_sh <= 4
        )
        gain = gains[b]
        query = rms(qkv[:, :head_size], gain[0:1, :])
        kvbuf[b, z, 0] = rms(qkv[:, head_size : 2 * head_size], gain[1:2, :])
        kvbuf[b, z, 1] = qkv[:, 2 * head_size :].astype(BF16)
        return query

    def attend(b, query):
        scale = head_size ** (-0.5)
        text = texts[b]

        def scores(keys):
            return (
                lax.dot_general(query, keys, (((1,), (1,)), ((), ())), preferred_element_type=F32)
                * scale
            )

        slots = text.shape[1]
        text_score = scores(text[0])
        spot = lax.broadcasted_iota(jnp.int32, (query.shape[0], slots), 1)
        text_score = jnp.where(spot < text_len[0], text_score, -1e30)
        top = jnp.max(text_score, axis=1, keepdims=True)

        def first(s, top):
            score = scores(kvbuf[b, s, 0])
            score_buf[s] = score
            return jnp.maximum(top, jnp.max(score, axis=1, keepdims=True))

        top = lax.fori_loop(0, n_patch, first, top, unroll=n_patch <= 4)
        expo = jnp.exp(text_score - top)
        total = jnp.sum(expo, axis=1, keepdims=True)
        mixed = jnp.dot(expo.astype(BF16), text[1], preferred_element_type=F32)

        def second(s, carry):
            total, mixed = carry
            expo = jnp.exp(score_buf[s] - top)
            return (
                total + jnp.sum(expo, axis=1, keepdims=True),
                mixed + jnp.dot(expo.astype(BF16), kvbuf[b, s, 1], preferred_element_type=F32),
            )

        total, mixed = lax.fori_loop(
            0, n_patch, second, (total, mixed), unroll=n_patch <= 4
        )
        return (mixed / total).astype(BF16)

    piece = rows // PARTS

    def rows_of(r):
        return pl.ds(r * piece, piece)

    def section_of(k):
        return lax.rem(x + 1 + k, n_sec)

    def pair_copy(b, r, k):
        o = section_of(k)
        src = psend.at[b, o * n_head + other, rows_of(r)]
        dst = pair.at[b, o, rows_of(r)]
        return remote(src, dst, pair_send.at[b, r, o], pair_recv.at[b, r, o], device(c_=other))

    def p_copy(b, r, k):
        o = section_of(k)
        src = psend.at[b, o * n_head + c, rows_of(r)]
        dst = pbuf.at[b, x, rows_of(r)]
        return remote(src, dst, p_send.at[b, r, o], p_recv.at[b, r, x], device(x_=o))

    def out_part(b, attn, s):
        wo = wos[b]
        if len(wo.shape) == 3:
            weight = wo[s]
        else:
            weight = wo[:, pl.ds(pl.multiple_of(s * cols, cols), cols)]
        return jnp.dot(attn, weight, preferred_element_type=F32).astype(BF16)

    def out_start(b, r, attn):
        for k in range(n_sec):
            s = section_of(k) * n_head + other
            psend[b, s, rows_of(r), :] = out_part(b, attn, s)
            pair_copy(b, r, k).start()
        for k in range(n_sec - 1):
            o = section_of(k)
            mine = out_part(b, attn, o * n_head + c).astype(F32)
            pair_copy(b, r, k).wait_recv()
            total = mine + pair[b, o, rows_of(r), :].astype(F32)
            psend[b, o * n_head + c, rows_of(r), :] = total.astype(BF16)
            p_copy(b, r, k).start()
        pbuf[b, x, rows_of(r), :] = out_part(b, attn, me)

    def out_wait(b, r):
        pair_copy(b, r, n_sec - 1).wait_recv()
        for k in range(n_sec - 1):
            o = section_of(k)
            remote(
                pbuf.at[b, o, rows_of(r)],
                pbuf.at[b, o, rows_of(r)],
                p_send.at[b, r, o],
                p_recv.at[b, r, o],
                device(c_=other),
            ).wait_recv()

    def attend_out(b, query):
        for r in range(PARTS):
            out_start(b, r, attend(b, query[r * piece : (r + 1) * piece]))

    def gated(b, at):
        total = pair[b, x, at, :].astype(F32)
        for o in range(n_sec):
            total += pbuf[b, o, at, :].astype(F32)
        return hids[b][at, :].astype(F32) + mod_row(b, 2, me) * total

    def ctrl_finish():
        for d in range(n_patch):
            if d * PARTS % n_patch == 0:
                out_wait(0, d * PARTS // n_patch)
            at = pl.ds(d * blk, blk)
            out0[at, :] = gated(0, at).astype(BF16)

    def b_copy(k):
        d = lax.rem(z + k, n_patch)
        return remote(blk_send.at[d], blk_buf.at[z], b_send.at[d], b_recv.at[z], device(z_=d))

    def equal(one, two):
        return (one == two).astype(F32)

    def relay_start():
        def block_for(d):
            def outer(j, block):
                def inner(i, found):
                    return found + equal(base_order[d * n_patch + i], ctrl_order[z * n_patch + j])

                found = lax.fori_loop(0, n_patch, inner, jnp.float32(0.0))
                at = pl.ds(pl.multiple_of(j * blk, blk), blk)
                return block + found * out0[at, :].astype(F32)

            return lax.fori_loop(0, n_patch, outer, jnp.zeros((blk, cols), F32)).astype(BF16)

        for k in range(1, n_patch):
            d = lax.rem(z + k, n_patch)
            blk_send[d] = block_for(d)
            b_copy(k).start()
        blk_buf[z] = block_for(z)

    def relay_wait():
        for k in range(1, n_patch):
            d = lax.rem(z + k, n_patch)
            remote(
                blk_send.at[d], blk_buf.at[d], b_send.at[d], b_recv.at[d], device(z_=d)
            ).wait_recv()

    def base_finish():
        for i in range(n_patch):
            at = pl.ds(i * blk, blk)

            def outer(s, block):
                def inner(j, found):
                    return found + equal(ctrl_order[s * n_patch + j], base_order[z * n_patch + i])

                found = lax.fori_loop(0, n_patch, inner, jnp.float32(0.0))
                return block + found * blk_buf[s].astype(F32)

            relaid = lax.fori_loop(0, n_patch, outer, jnp.zeros((blk, cols), F32))
            if i * PARTS % n_patch == 0:
                out_wait(1, i * PARTS // n_patch)
            out1[at, :] = (gated(1, at) + relaid).astype(BF16)

    barrier = pltpu.get_barrier_semaphore()
    partners = [device(g_=1 - g)]
    partners += [device(z_=lax.rem(z + k, n_patch)) for k in range(1, n_patch)]
    partners += [device(x_=section_of(k)) for k in range(n_sec - 1)]
    partners.append(device(c_=other))
    for partner in partners:
        pl.semaphore_signal(
            barrier, inc=1, device_id=partner, device_id_type=pl.DeviceIdType.MESH
        )
    pl.semaphore_wait(barrier, len(partners))

    last = n_patch - 1
    chain_start(w_copy, 0, 0)
    hid_start(0)
    chain_start(kv_copy, 0, 0)
    chain_start(w_copy, 1, 0)
    hid_start(1)
    for load in loads:
        load.wait()
    for b in range(2):
        hbuf[b, me] = hids[b][...]
        for part in range(2):
            wbuf[b, z, part] = ws[b][:, part]
    hid_forward(0)
    w_arrive(0, 0)
    kv_arrive(0, 0)
    for t in range(1, last - 1):
        w_arrive(0, t)
        kv_arrive(0, t)
    hid_forward(1)
    w_arrive(1, 0)
    chain_start(kv_copy, 1, 0)
    hid_wait(0)
    normalize(0)
    w_arrive(0, last - 1)
    w_wait(0)
    query = project(0)
    for t in range(1, last - 1):
        w_arrive(1, t)
    kv_arrive(0, last - 1)
    attend_out(0, query)
    for t in range(last - 1):
        kv_arrive(1, t)
    hid_wait(1)
    normalize(1)
    w_arrive(1, last - 1)
    ctrl_finish()
    relay_start()
    w_wait(1)
    query = project(1)
    kv_arrive(1, last - 1)
    attend_out(1, query)
    relay_wait()
    base_finish()

    for b in range(2):
        for k in range(n_sec):
            hid_copy(b, k).wait_send()
        for k in range(1, n_sec):
            hid_fwd_copy(b, k).wait_send()
        for t in range(last):
            for side in range(2):

                @pl.when(sends(t, side))
                def _():
                    w_copy(b, t, side).wait_send()
                    kv_copy(b, t, side).wait_send()

        for k in range(1, n_patch):
            y_copy(b, lax.rem(z + k, n_patch)).wait_send()
        for k in range(n_sec - 1):
            for r in range(PARTS):
                p_copy(b, r, k).wait_send()
        for k in range(n_sec):
            for r in range(PARTS):
                pair_copy(b, r, k).wait_send()
    for k in range(1, n_patch):
        b_copy(k).wait_send()


def local(
    sizes,
    ctrl_hidden,
    base_hidden,
    ctrl_qkv_weight,
    base_qkv_weight,
    ctrl_out_weight,
    base_out_weight,
    ctrl_mod,
    base_mod,
    ctrl_qk_gain,
    base_qk_gain,
    ctrl_stale,
    base_stale,
    ctrl_text,
    base_text,
    ctrl_order,
    base_order,
    text_len,
):
    n_groups, n_patch, n_sec, n_head = sizes
    n_sh = n_sec * n_head
    rows, cols = ctrl_hidden.shape
    w_rows, _, head_size = ctrl_qkv_weight.shape
    blk = rows // n_patch

    def halves(weight):
        return weight.transpose(1, 0, 2).reshape(3, 2, w_rows // 2, head_size)

    def by_columns(weight):
        if cols % 128 == 0:
            return weight
        return weight.reshape(weight.shape[0], n_sh, cols).transpose(1, 0, 2)

    def mod_rows(mod):
        return mod if cols % 128 == 0 else mod.reshape(3 * n_sh, 1, cols)

    operands = (
        ctrl_hidden,
        base_hidden,
        halves(ctrl_qkv_weight),
        halves(base_qkv_weight),
        by_columns(ctrl_out_weight),
        by_columns(base_out_weight),
        mod_rows(ctrl_mod),
        mod_rows(base_mod),
        ctrl_qk_gain,
        base_qk_gain,
        ctrl_stale,
        base_stale,
        ctrl_text,
        base_text,
    )
    held = operands[:10] + operands[12:]
    smem = pl.BlockSpec(memory_space=pltpu.SMEM)
    vmem = pl.BlockSpec(memory_space=pltpu.VMEM)
    hbm = pl.BlockSpec(memory_space=pltpu.HBM)
    dma = pltpu.SemaphoreType.DMA
    out = jax.ShapeDtypeStruct((rows, cols), BF16)
    return pl.pallas_call(
        functools.partial(kernel, sizes),
        out_shape=(out, out),
        in_specs=[smem] * 3 + [hbm] * 14,
        out_specs=(vmem, vmem),
        scratch_shapes=[
            pltpu.VMEM((2, n_sh, rows, cols), BF16),
            pltpu.VMEM((2, n_patch, 2, 3, w_rows // 2, head_size), BF16),
            pltpu.VMEM((2, n_patch, 2, rows, head_size), BF16),
            pltpu.VMEM((2, n_sh, rows, cols), BF16),
            pltpu.VMEM((2, n_sec, rows, cols), BF16),
            pltpu.VMEM((2, n_sec, rows, cols), BF16),
            pltpu.VMEM((n_sh, rows, cols), BF16),
            pltpu.VMEM((n_patch, rows // PARTS, rows), F32),
            pltpu.VMEM((n_patch, blk, cols), BF16),
            pltpu.VMEM((n_patch, blk, cols), BF16),
            dma((2, n_sec)),
            dma((2, n_sec)),
            dma((2, n_sh)),
            dma((2, 2, n_patch)),
            dma((2, n_patch)),
            dma((2, n_patch)),
            dma((2, n_patch)),
            dma((2, 2, n_patch)),
            dma((2, n_patch)),
            dma((2, PARTS, n_sec)),
            dma((2, PARTS, n_sec)),
            dma((2, PARTS, n_sec)),
            dma((2, PARTS, n_sec)),
            dma((n_patch,)),
            dma((n_patch,)),
            dma((len(held),)),
        ]
        + [pltpu.VMEM(array.shape, array.dtype) for array in held],
        compiler_params=pltpu.CompilerParams(
            collective_id=0, has_side_effects=True, vmem_limit_bytes=56 * 1024 * 1024
        ),
    )(
        text_len,
        ctrl_order,
        base_order,
        *operands,
    )


def solution(mesh):
    sizes = tuple(mesh.shape[name] for name in ("groups", "patch", "section", "head"))
    in_specs = (
        P(("groups", "patch"), ("section", "head")),
        P(("groups", "patch"), ("section", "head")),
        P("patch", None, ("section", "head")),
        P("patch", None, ("section", "head")),
        P(("section", "head"), None),
        P(("section", "head"), None),
        P(),
        P(),
        P(),
        P(),
        P(None, ("groups", "patch"), ("section", "head")),
        P(None, ("groups", "patch"), ("section", "head")),
        P(None, "groups", ("section", "head")),
        P(None, "groups", ("section", "head")),
        P(),
        P(),
        P("groups"),
    )
    out_specs = (
        P(("groups", "patch"), ("section", "head")),
        P(("groups", "patch"), ("section", "head")),
    )
    return jax.shard_map(
        functools.partial(local, sizes),
        mesh=mesh,
        in_specs=in_specs,
        out_specs=out_specs,
        check_vma=False,
    )
```
